32 devices in a mesh: dp: 2 (over core), row: 4 (over y, x), col: 4 (over z).
Axes of the slice: x: 2, y: 2, z: 4, core: 2. Of those that a mesh axis runs over, the one named last changes fastest.
Arguments:
- tokens: bfloat16 [1536, 8192], P('dp', 'row'), may hold values from -6 to 6
- out_grad: bfloat16 [1536, 8192], P('dp', 'row'), may hold values from -6 to 6
- gate_weight: bfloat16 [8192, 14336], P('row', 'col'), may hold values from -0.0625 to 0.0625
- up_weight: bfloat16 [8192, 14336], P('row', 'col'), may hold values from -0.0625 to 0.0625
- down_weight: bfloat16 [14336, 8192], P('col', 'row'), may hold values from -0.046875 to 0.046875
- gate_mask: int32 [64, 112], P('row', 'col'), may hold values from 0 to 1, as said below
- up_mask: int32 [64, 112], P('row', 'col'), may hold values from 0 to 1, as said below
- down_mask: int32 [112, 64], P('col', 'row'), may hold values from 0 to 1, as said below
Outputs:
- output: bfloat16 [1536, 8192], P(('dp', 'col'), 'row')
- token_grad: bfloat16 [1536, 8192], P(('dp', 'col'), 'row')
- gate_grad: bfloat16 [8192, 14336], P('row', 'col')
- up_grad: bfloat16 [8192, 14336], P('row', 'col')
- down_grad: bfloat16 [14336, 8192], P('col', 'row')
The draws below stay inside these ranges and needn't reach their ends.
Inputs may be any that keep to these rules, and one draw needn't show every extreme that they name: `gate_mask`: one keep flag for each 128 x 128 block of the matrix; the share kept differs from block row to block row. `up_mask`: one keep flag for each 128 x 128 block of the matrix; the share kept differs from block row to block row. `down_mask`: one keep flag for each 128 x 128 block of the matrix; the share kept differs from block column to block column.
All inputs are finite; a program needn't handle non-finite values.
Results may differ from the reference program's by a relative error of at most 0.029.
Values may be sent and summed in bfloat16 or wider, within the bound.
No kernel may reach another device: no remote copies, remote signals or barrier semaphores. Data moves between devices by JAX's collectives and lax.ppermute only.
A program may use at most 256 MiB of HBM per device.

```python
import jax
import jax.numpy as jnp
from jax import lax

D = 8192
FF = 14336
BLOCK = 128
TOK = 768
TOKENS = 1536
N_DP = 2
N_ROW = 4
N_COL = 4


def keep_flags(key, height, breadth, salt_value):
    folded = jax.random.fold_in(key, salt_value)
    first_key, second_key = jax.random.split(folded)
    keep_level = jax.random.randint(first_key, (height, 1), 1, 8)
    ballots = jax.random.randint(second_key, (height, breadth), 0, 10)
    return (ballots < keep_level).astype(jnp.int32)


def draw_gate_mask(key, part):
    return keep_flags(key, D // BLOCK, FF // BLOCK, 11)


def draw_up_mask(key, part):
    return keep_flags(key, D // BLOCK, FF // BLOCK, 12)


def draw_down_mask(key, part):
    return keep_flags(key, D // BLOCK, FF // BLOCK, 13).T


def level_of(rng, shape, cuts, least, largest):
    loudness, own = 1.0, jax.random.fold_in(rng, 6)
    for axis_at, blocks in cuts:
        heights = jnp.exp(jax.random.uniform(jax.random.fold_in(own, axis_at), (blocks,), jnp.float32, least / len(cuts), largest / len(cuts)))
        loudness = loudness * jnp.repeat(heights, shape[axis_at] // blocks).reshape([-1 if axis == axis_at else 1 for axis in range(len(shape))])
    return loudness


def bell_draw(own_key, dims, spread, bound, cuts=(), kind=jnp.bfloat16):
    loudness = level_of(own_key, dims, cuts, -0.22, 0.18) if cuts else 1.0
    values = jax.random.normal(own_key, dims, jnp.float32) * spread * loudness
    return jnp.minimum(jnp.maximum(values, -bound), bound).astype(kind)


def setup_inputs(seed: int = 0) -> dict:
    key_list = jax.random.split(jax.random.key(seed), 9)
    tokens = bell_draw(key_list[0], (TOKENS, D), 1.0, 6.0, ((0, 2), (1, 4)))
    out_grad = bell_draw(key_list[1], (TOKENS, D), 1.0, 6.0, ((0, 2), (1, 4)))
    gate_weight = bell_draw(key_list[2], (D, FF), D ** -0.5, 0.0625, ((0, 4), (1, 4)))
    up_weight = bell_draw(key_list[3], (D, FF), D ** -0.5, 0.0625, ((0, 4), (1, 4)))
    down_weight = bell_draw(key_list[4], (FF, D), FF ** -0.5, 0.046875, ((0, 4), (1, 4)))
    gate_mask = draw_gate_mask(jax.random.fold_in(key_list[8], 71), 0)
    up_mask = draw_up_mask(jax.random.fold_in(key_list[8], 71), 0)
    down_mask = draw_down_mask(jax.random.fold_in(key_list[8], 71), 0)
    return dict(tokens=tokens, out_grad=out_grad, gate_weight=gate_weight, up_weight=up_weight, down_weight=down_weight, gate_mask=gate_mask, up_mask=up_mask, down_mask=down_mask)


def expand(mask_tile):
    return jnp.repeat(jnp.repeat(mask_tile, BLOCK, axis=0), BLOCK, axis=1)


def tile_sum(pairs, parts):
    rows_out = pairs[0][0].shape[0]
    cols_out = pairs[0][1].shape[1]
    width = pairs[0][0].shape[1] // parts

    def advance(running, tile_index):
        partial_sum = jnp.zeros((rows_out, cols_out), jnp.float32)
        for left_side, right_side in pairs:
            left_piece = lax.dynamic_slice_in_dim(left_side, tile_index * width, width, 1)
            right_piece = lax.dynamic_slice_in_dim(right_side, tile_index * width, width, 0)
            partial_sum = partial_sum + jnp.dot(left_piece, right_piece, preferred_element_type=jnp.float32)
        rounded = lax.optimization_barrier(partial_sum.astype(jnp.bfloat16)).astype(jnp.float32)
        return running + rounded, None

    running, unused_out = lax.scan(advance, jnp.zeros((rows_out, cols_out), jnp.float32), jnp.arange(parts, dtype=jnp.int32))
    return running


def contract_rows(left_side, right_side):
    return lax.dot_general(left_side, right_side, (((0,), (0,)), ((), ())), preferred_element_type=jnp.float32)


def reference(tokens, out_grad, gate_weight, up_weight, down_weight, gate_mask, up_mask, down_mask):
    gate_keep = expand(gate_mask).astype(jnp.float32)
    up_keep = expand(up_mask).astype(jnp.float32)
    down_keep = expand(down_mask).astype(jnp.float32)
    gate_eff = gate_weight * gate_keep.astype(jnp.bfloat16)
    up_eff = up_weight * up_keep.astype(jnp.bfloat16)
    down_eff = down_weight * down_keep.astype(jnp.bfloat16)
    down_trans = down_eff.T
    gate_trans = gate_eff.T
    up_trans = up_eff.T
    outputs = []
    token_grads = []
    gate_total = jnp.zeros(gate_weight.shape, jnp.float32)
    up_total = jnp.zeros(up_weight.shape, jnp.float32)
    down_total = jnp.zeros(down_weight.shape, jnp.float32)
    for group in range(N_DP):
        group_in = tokens[group * TOK:(group + 1) * TOK]
        group_dy = out_grad[group * TOK:(group + 1) * TOK]
        gate_pre = tile_sum([(group_in, gate_eff)], N_ROW)
        up_pre = tile_sum([(group_in, up_eff)], N_ROW)
        gate_sig = jax.nn.sigmoid(gate_pre)
        silu_gate = gate_pre * gate_sig
        hidden = (silu_gate * up_pre).astype(jnp.bfloat16)
        outputs.append(tile_sum([(hidden, down_eff)], N_COL).astype(jnp.bfloat16))
        back = tile_sum([(group_dy, down_trans)], N_ROW)
        gate_deriv = (back * up_pre * gate_sig * (1.0 + gate_pre * (1.0 - gate_sig))).astype(jnp.bfloat16)
        up_deriv = (back * silu_gate).astype(jnp.bfloat16)
        token_grads.append(tile_sum([(gate_deriv, gate_trans), (up_deriv, up_trans)], N_COL).astype(jnp.bfloat16))
        gate_local = (contract_rows(group_in, gate_deriv) * gate_keep).astype(jnp.bfloat16)
        up_local = (contract_rows(group_in, up_deriv) * up_keep).astype(jnp.bfloat16)
        down_local = (contract_rows(hidden, group_dy) * down_keep).astype(jnp.bfloat16)
        gate_total = gate_total + gate_local.astype(jnp.float32)
        up_total = up_total + up_local.astype(jnp.float32)
        down_total = down_total + down_local.astype(jnp.float32)
    output = jnp.concatenate(outputs, axis=0)
    token_grad = jnp.concatenate(token_grads, axis=0)
    return (output, token_grad, gate_total.astype(jnp.bfloat16), up_total.astype(jnp.bfloat16), down_total.astype(jnp.bfloat16))
```

```python
import functools

import jax
import jax.numpy as jnp
from jax import lax
from jax.experimental import pallas as pl
from jax.experimental.pallas import tpu as pltpu
from jax.sharding import PartitionSpec as P

BLOCK = 128
TILE = 512
F32 = jnp.float32
BF16 = jnp.bfloat16
ANY = pl.BlockSpec(memory_space=pl.ANY)
SMEM = pl.BlockSpec(memory_space=pltpu.SMEM)


def expand(mask_tile):
    return jnp.repeat(jnp.repeat(mask_tile, BLOCK, axis=0), BLOCK, axis=1)


def dot(left_side, right_side, left_dim=1, right_dim=0):
    return lax.dot_general(
        left_side, right_side, (((left_dim,), (right_dim,)), ((), ())), preferred_element_type=F32
    )


def contract_rows(left_side, right_side):
    return dot(left_side, right_side, 0, 0)


def contract_cols(left_side, right_side):
    return dot(left_side, right_side, 1, 1)


def pair_x(array):
    return lax.ppermute(array, "row", [(i, i ^ 1) for i in range(4)])


def pair_y(array):
    return lax.ppermute(array, "row", [(i, i ^ 2) for i in range(4)])


def pair_z(array, bit):
    return lax.ppermute(array, "col", [(i, i ^ bit) for i in range(4)])


def swap_dp(array):
    return lax.ppermute(array, "dp", [(0, 1), (1, 0)])


def cat(parts, axis=0):
    return lax.concatenate(parts, axis)


def shape_of(*dims):
    return jax.ShapeDtypeStruct(dims, BF16)


def full(array):
    return pl.BlockSpec(array.shape, lambda *at: (0,) * array.ndim)


class Runner:
    def __init__(self):
        self.last = None

    def __call__(self, kernel, grid, args, in_specs, out_shape, out_specs, scratch=(), flops=0, alias=None):
        extra = [] if self.last is None else [self.last]
        count = len(args)

        def wrapped(*refs):
            kernel(*refs[:count], *refs[count + len(extra) :])

        outs = pl.pallas_call(
            wrapped,
            grid=grid,
            in_specs=list(in_specs) + [ANY] * len(extra),
            out_specs=out_specs,
            out_shape=out_shape,
            scratch_shapes=list(scratch),
            input_output_aliases=alias or {},
            compiler_params=pltpu.CompilerParams(vmem_limit_bytes=56 * 1024 * 1024),
            cost_estimate=pl.CostEstimate(flops=flops, bytes_accessed=1 << 20, transcendentals=0),
        )(*args, *extra)
        self.last = outs[0] if isinstance(outs, (tuple, list)) else outs
        return outs


def masked(scr, weight_ref, mask_ref, row_at, col_at):
    rows, cols = weight_ref.shape
    for r in range(rows // BLOCK):
        for c in range(cols // BLOCK):
            at = (slice(r * BLOCK, (r + 1) * BLOCK), slice(c * BLOCK, (c + 1) * BLOCK))
            tile = weight_ref[at]
            scr[at] = jnp.where(mask_ref[row_at + r, col_at + c] > 0, tile, jnp.zeros_like(tile))
    return scr[...]


def store_masked(out_ref, row, grad, mask_ref, row_at, col_at):
    rows, cols = grad.shape
    for r in range(0, rows, BLOCK):
        for c in range(0, cols, BLOCK):
            tile = grad[r : r + BLOCK, c : c + BLOCK]
            kept = mask_ref[row_at + r // BLOCK, col_at + c // BLOCK] > 0
            out_ref[row + r : row + r + BLOCK, c : c + BLOCK] = jnp.where(kept, tile, jnp.zeros_like(tile))


def run_gate_up(run, tokens, gate_weight, up_weight, gate_mask, up_mask, place, lo, hi):
    count, width = tokens.shape
    n, base, share, cols = (hi - lo) // TILE, lo // TILE, count // 4, hi - lo

    def kernel(x_ref, wg_ref, wu_ref, mg_ref, mu_ref, place_ref, s0, s1, s2, g3, u3, w_scr, scr):
        part, j = pl.program_id(0), pl.program_id(1)

        def work(w_ref, m_ref, last):
            weight = masked(w_scr, w_ref, m_ref, 0, (base + j) * (TILE // BLOCK))
            scr[...] = dot(x_ref[...], weight).astype(BF16)
            for k, out in enumerate((s0, s1, s2, last)):
                out[...] = scr[pl.ds(pl.multiple_of((place_ref[0] ^ k) * share, share), share), :]

        pl.when(part == 0)(lambda: work(wg_ref, mg_ref, g3))
        pl.when(part == 1)(lambda: work(wu_ref, mu_ref, u3))

    def first(p, j):
        return (0, jnp.where(p == 0, j, n - 1))

    def second(p, j):
        return (0, jnp.where(p == 0, 0, j))

    both = pl.BlockSpec((share, TILE), lambda p, j: (0, p * n + j))
    return run(
        kernel,
        (2, n),
        (tokens, gate_weight, up_weight, gate_mask, up_mask, place),
        [
            full(tokens),
            pl.BlockSpec((width, TILE), lambda p, j: (0, base + jnp.where(p == 0, j, n - 1))),
            pl.BlockSpec((width, TILE), lambda p, j: (0, base + jnp.where(p == 0, 0, j))),
            SMEM,
            SMEM,
            SMEM,
        ],
        [shape_of(share, 2 * cols)] * 3 + [shape_of(share, cols)] * 2,
        [both] * 3 + [pl.BlockSpec((share, TILE), first), pl.BlockSpec((share, TILE), second)],
        [pltpu.VMEM((width, TILE), BF16), pltpu.VMEM((count, TILE), BF16)],
        flops=4 * count * width * cols,
    )


def run_combine(run, one, two, got_gate, got_up):
    share, cols = got_gate.shape

    def kernel(one_ref, two_ref, gate_ref, up_ref, one_out, two_out):
        one_out[...] = (one_ref[...].astype(F32) + up_ref[...].astype(F32)).astype(BF16)
        two_out[...] = (two_ref[...].astype(F32) + gate_ref[...].astype(F32)).astype(BF16)

    rows = share // 2
    left = pl.BlockSpec((rows, cols), lambda j: (j, 0))
    right = pl.BlockSpec((rows, cols), lambda j: (j, 1))
    return run(
        kernel,
        (2,),
        (one, two, got_gate, got_up),
        [right, left, left, left],
        [shape_of(*one.shape)] * 2,
        [right, left],
        alias={0: 0, 1: 1},
    )


def run_back(run, out_grad, down_weight, down_mask, lo, hi):
    count, width = out_grad.shape
    n, base = (hi - lo) // TILE, lo // TILE

    def kernel(dy_ref, wd_ref, md_ref, out_ref, w_scr):
        j = pl.program_id(0)
        weight = masked(w_scr, wd_ref, md_ref, (base + j) * (TILE // BLOCK), 0)
        out_ref[...] = dot(dy_ref[...], weight, 1, 1).astype(BF16)

    return run(
        kernel,
        (n,),
        (out_grad, down_weight, down_mask),
        [full(out_grad), pl.BlockSpec((TILE, width), lambda j: (base + j, 0)), SMEM],
        shape_of(count, hi - lo),
        pl.BlockSpec((count, TILE), lambda j: (0, j)),
        [pltpu.VMEM((TILE, width), BF16)],
        flops=2 * count * width * (hi - lo),
    )


def add_three(refs, col, width):
    first, second, third = (ref[:, col : col + width].astype(F32) for ref in refs)
    return first + second + third


STEP = 256


def run_hidden(run, sums):
    share = sums[0][0].shape[0]
    widths = [group[0].shape[1] // 2 for group in sums]
    rows = share // 4

    def kernel(*refs):
        out_ref, start = refs[-1], 0
        for i, cols in enumerate(widths):
            group = refs[3 * i : 3 * i + 3]
            for at in range(0, cols, STEP):
                gate, up = add_three(group, at, STEP), add_three(group, cols + at, STEP)
                out_ref[:, start + at : start + at + STEP] = (gate * jax.nn.sigmoid(gate) * up).astype(BF16)
            start += cols

    flat = [array for group in sums for array in group]
    return run(
        kernel,
        (share // rows,),
        flat,
        [pl.BlockSpec((rows, array.shape[1]), lambda j: (j, 0)) for array in flat],
        shape_of(share, sum(widths)),
        pl.BlockSpec((rows, sum(widths)), lambda j: (j, 0)),
    )


def run_derivs(run, sums, back, back_at, row_lo, row_hi):
    cols = sums[0].shape[1] // 2
    rows = 32
    base = row_lo // rows

    def kernel(s0, s1, s2, back_ref, out_ref):
        for at in range(0, cols, STEP):
            gate, up = add_three((s0, s1, s2), at, STEP), add_three((s0, s1, s2), cols + at, STEP)
            grad = back_ref[:, back_at + at : back_at + at + STEP].astype(F32)
            sig = jax.nn.sigmoid(gate)
            silu = gate * sig
            out_ref[:, at : at + STEP] = (grad * up * (sig + silu * (1.0 - sig))).astype(BF16)
            out_ref[:, cols + at : cols + at + STEP] = (grad * silu).astype(BF16)

    return run(
        kernel,
        ((row_hi - row_lo) // rows,),
        (*sums, back),
        [pl.BlockSpec((rows, array.shape[1]), lambda j: (base + j, 0)) for array in (*sums, back)],
        shape_of(row_hi - row_lo, 2 * cols),
        pl.BlockSpec((rows, 2 * cols), lambda j: (j, 0)),
    )


def run_assemble(run, parts, place):
    rows, width = parts[0].shape
    half = rows // 2

    def kernel(*refs):
        place_ref, out_ref = refs[5], refs[6]
        for k, part in enumerate(refs[:5]):
            at = (place_ref[0] ^ min(k, 3)) * rows + (half if k == 4 else 0)
            out_ref[pl.ds(pl.multiple_of(at, half), part.shape[0]), :] = part[...]

    return run(
        kernel,
        (width // TILE,),
        (*parts, place),
        [pl.BlockSpec((part.shape[0], TILE), lambda j: (0, j)) for part in parts] + [SMEM],
        shape_of(4 * rows, width),
        pl.BlockSpec((4 * rows, TILE), lambda j: (0, j)),
    )


def gather_rows(run, own, place):
    half = own.shape[0] // 2
    got_x, got_y = pair_x(own), pair_y(own)
    far = [pair_y(got_x[:half]), pair_x(got_y[half:])]
    return lambda: run_assemble(run, (own, got_x, got_y, *far), place)


def write_col_halves(total, place_ref, keep_ref, send_ref, scr):
    rows = total.shape[0] // 4
    scr[...] = total.astype(BF16)
    low = place_ref[2] & 1
    for i in range(2):
        keep_ref[i * rows : (i + 1) * rows] = scr[pl.ds(pl.multiple_of((2 * i + low) * rows, rows), rows), :]
        send_ref[i * rows : (i + 1) * rows] = scr[pl.ds(pl.multiple_of((2 * i + 1 - low) * rows, rows), rows), :]


def col_halves(count, width):
    spec = pl.BlockSpec((count // 2, TILE), lambda j: (0, j))
    return [shape_of(count // 2, width)] * 2, [spec] * 2, [pltpu.VMEM((count, TILE), BF16)]


def col_scatter(keep, send, col):
    rows = keep.shape[0] // 2
    total = (keep.astype(F32) + pair_z(send, 1).astype(F32)).astype(BF16)
    high = col // 2
    got = pair_z(lax.dynamic_slice_in_dim(total, (1 - high) * rows, rows, 0), 2)
    mine = lax.dynamic_slice_in_dim(total, high * rows, rows, 0)
    return (mine.astype(F32) + got.astype(F32)).astype(BF16)


def run_output(run, hiddens, down_weight, down_mask, place):
    count = hiddens[0].shape[0]
    hidden_units, width = down_weight.shape

    def kernel(*refs):
        h_refs = refs[: len(hiddens)]
        wd_ref, md_ref, place_ref, keep_ref, send_ref, scr, w_scr = refs[len(hiddens) :]
        weight = masked(w_scr, wd_ref, md_ref, 0, pl.program_id(0) * (TILE // BLOCK))
        total, at = None, 0
        for h_ref in h_refs:
            cols = h_ref.shape[1]
            term = dot(h_ref[...], weight[at : at + cols])
            total, at = term if total is None else total + term, at + cols
        write_col_halves(total, place_ref, keep_ref, send_ref, scr)

    shapes, specs, scratch = col_halves(count, width)
    return run(
        kernel,
        (width // TILE,),
        (*hiddens, down_weight, down_mask, place),
        [full(h) for h in hiddens] + [pl.BlockSpec((hidden_units, TILE), lambda j: (0, j)), SMEM, SMEM],
        shapes,
        specs,
        scratch + [pltpu.VMEM((hidden_units, TILE), BF16)],
        flops=2 * count * hidden_units * width,
    )


def run_token_terms(run, derivs, gate_weight, up_weight, gate_mask, up_mask, pieces):
    count = derivs[0].shape[0]
    width = gate_weight.shape[0]
    widths = [d.shape[1] // 2 for d in derivs]
    cols, share = sum(widths), count // 4
    rows = share // pieces

    def kernel(*refs):
        d_refs = refs[: len(derivs)]
        wg_ref, wu_ref, mg_ref, mu_ref = refs[len(derivs) : len(derivs) + 4]
        outs = refs[len(derivs) + 4 : -2]
        row_at = pl.program_id(0) * (TILE // BLOCK)
        gate = masked(refs[-2], wg_ref, mg_ref, row_at, 0)
        up = masked(refs[-1], wu_ref, mu_ref, row_at, 0)
        total, at = None, 0
        for d_ref, here in zip(d_refs, widths):
            term = dot(d_ref[:, :here], gate[:, at : at + here], 1, 1)
            term = term + dot(d_ref[:, here:], up[:, at : at + here], 1, 1)
            total, at = term if total is None else total + term, at + here
        for t, out in enumerate(outs):
            for owner in range(4):
                start = owner * share + t * rows
                out[owner * rows : (owner + 1) * rows] = total[start : start + rows]

    weight_spec = pl.BlockSpec((TILE, cols), lambda j: (j, 0))
    return run(
        kernel,
        (width // TILE,),
        (*derivs, gate_weight, up_weight, gate_mask, up_mask),
        [full(d) for d in derivs] + [weight_spec] * 2 + [SMEM] * 2,
        [jax.ShapeDtypeStruct((4 * rows, width), F32)] * pieces,
        [pl.BlockSpec((4 * rows, TILE), lambda j: (0, j))] * pieces,
        [pltpu.VMEM((TILE, cols), BF16)] * 2,
        flops=4 * count * cols * width,
    )


def run_token_grad(run, deriv, terms, gate_weight, up_weight, gate_mask, up_mask, place, lo):
    count = deriv.shape[0]
    width, cols = gate_weight.shape[0], deriv.shape[1] // 2
    n = cols // TILE

    def kernel(*refs):
        d_ref, terms_ref = refs[:2]
        mg_ref, mu_ref, place_ref, keep_ref, send_ref, scr, w_scr = refs[2 + 2 * n :]
        row_at = pl.program_id(0) * (TILE // BLOCK)
        total = terms_ref[...]
        for i in range(2 * n):
            m_ref = mg_ref if i < n else mu_ref
            weight = masked(w_scr.at[i], refs[2 + i], m_ref, row_at, (lo + (i % n) * TILE) // BLOCK)
            total = total + dot(d_ref[:, i * TILE : (i + 1) * TILE], weight, 1, 1)
        write_col_halves(total, place_ref, keep_ref, send_ref, scr)

    shapes, specs, scratch = col_halves(count, width)
    weight_specs = [pl.BlockSpec((TILE, TILE), functools.partial(lambda q, j: (j, q), lo // TILE + q)) for q in range(n)]
    return run(
        kernel,
        (width // TILE,),
        (deriv, terms, *[gate_weight] * n, *[up_weight] * n, gate_mask, up_mask, place),
        [full(deriv), pl.BlockSpec((count, TILE), lambda j: (0, j))] + weight_specs * 2 + [SMEM] * 3,
        shapes,
        specs,
        scratch + [pltpu.VMEM((2 * n, TILE, TILE), BF16)],
        flops=4 * count * cols * width,
    )


def both_groups(dst, own, other, place_ref, count):
    share = count // 4
    for refs, group in ((own, place_ref[1]), (other, 1 - place_ref[1])):
        if len(refs) == 1:
            dst[pl.ds(pl.multiple_of(group * count, count), count), :] = refs[0][...]
            continue
        rows = share // len(refs)
        for t, ref in enumerate(refs):
            for owner in range(4):
                at = pl.multiple_of(group * count + owner * share + t * rows, rows)
                dst[pl.ds(at, rows), :] = ref[owner * rows : (owner + 1) * rows]


def run_down_grad(run, hid, hid_other, dy_all, down_mask, place, lo, hidden_units, so_far):
    count, cols = hid.shape
    width = dy_all.shape[1]
    n, base = cols // TILE, lo // TILE
    more = [] if so_far is None else [so_far]

    def kernel(*refs):
        h_ref, ho_ref, dy_ref, md_ref, place_ref = refs[:5]
        out_ref, h_all = refs[-2:]
        j = pl.program_id(0)
        both_groups(h_all, (h_ref,), (ho_ref,), place_ref, count)
        left = h_all[...]
        for at in range(0, width, 512):
            grad = dot(left, dy_ref[:, at : at + 512], 0, 0).astype(BF16)
            store_masked(out_ref.at[:, at : at + 512], 0, grad, md_ref, (base + j) * (TILE // BLOCK), at // BLOCK)

    return run(
        kernel,
        (n,),
        (hid, hid_other, dy_all, down_mask, place, *more),
        [pl.BlockSpec((count, TILE), lambda j: (0, j))] * 2 + [full(dy_all), SMEM, SMEM] + [ANY] * len(more),
        shape_of(hidden_units, width),
        pl.BlockSpec((TILE, width), lambda j: (base + j, 0)),
        [pltpu.VMEM((2 * count, TILE), BF16)],
        flops=4 * count * width * cols,
        alias={5: 0} if more else None,
    )


def run_weight_grads(run, xt_all, derivs, others, masks, place, lo, hidden_units, so_far):
    width, all_count = xt_all.shape
    count = all_count // 2
    cols = derivs[0].shape[1] // 2
    n, base, parts = cols // TILE, lo // TILE, len(derivs)
    more = [] if so_far is None else list(so_far)

    def kernel(*refs):
        xt_ref, rest = refs[0], refs[1:]
        own_gate, own_up = rest[:parts], rest[parts : 2 * parts]
        other_gate, other_up = rest[2 * parts : 3 * parts], rest[3 * parts : 4 * parts]
        mg_ref, mu_ref, place_ref = rest[4 * parts : 4 * parts + 3]
        gate_out, up_out, d_all = rest[-3:]
        col_at = (base + pl.program_id(0)) * (TILE // BLOCK)
        for own, other, m_ref, out in (
            (own_gate, other_gate, mg_ref, gate_out),
            (own_up, other_up, mu_ref, up_out),
        ):
            both_groups(d_all, own, other, place_ref, count)
            right = d_all[...]
            for at in range(0, width, 512):
                grad = dot(xt_ref[at : at + 512], right).astype(BF16)
                store_masked(out, at, grad, m_ref, at // BLOCK, col_at)

    gate_specs = [pl.BlockSpec((d.shape[0], TILE), lambda j: (0, j)) for d in derivs]
    up_specs = [pl.BlockSpec((d.shape[0], TILE), lambda j: (0, n + j)) for d in derivs]
    args = (xt_all, *derivs, *derivs, *others, *others, *masks, place, *more)
    return run(
        kernel,
        (n,),
        args,
        [full(xt_all)] + (gate_specs + up_specs) * 2 + [SMEM] * 3 + [ANY] * len(more),
        [shape_of(width, hidden_units)] * 2,
        [pl.BlockSpec((width, TILE), lambda j: (0, base + j))] * 2,
        [pltpu.VMEM((all_count, TILE), BF16)],
        flops=8 * count * width * cols,
        alias={len(args) - 2: 0, len(args) - 1: 1} if more else None,
    )


def fast_body(tokens, out_grad, gate_weight, up_weight, down_weight, gate_mask, up_mask, down_mask):
    run = Runner()
    row, dp, col = (lax.axis_index(name) for name in ("row", "dp", "col"))
    place = jnp.stack([row, dp, col]).astype(jnp.int32)
    count, width = tokens.shape
    share = count // 4
    hidden_units = gate_weight.shape[1]
    masks = (gate_mask, up_mask)
    tiles = hidden_units // TILE
    edges = [0, tiles * 2 // 7 * TILE, tiles * 4 // 7 * TILE, hidden_units]
    pieces = 3
    rows = share // pieces

    def gate_up(i):
        parts = run_gate_up(run, tokens, gate_weight, up_weight, *masks, place, edges[i], edges[i + 1])
        return parts, pair_x(parts[3]), pair_y(parts[4])

    def combine(parts, got_gate, got_up):
        one, two = run_combine(run, parts[1], parts[2], got_gate, got_up)
        return parts[0], pair_x(one), pair_y(two)

    def back(lo, hi):
        part = run_back(run, out_grad, down_weight, down_mask, lo, hi)
        return lax.psum_scatter(part, "row", scatter_dimension=0, tiled=True)

    def hidden(groups):
        return lax.all_gather(run_hidden(run, groups), "row", axis=0, tiled=True)

    def by_group(own):
        other = swap_dp(own)
        return jnp.where(dp == 0, cat([own, other]), cat([other, own]))

    first = gate_up(0)
    back_0 = back(edges[0], edges[1])
    second = gate_up(1)
    sums_0 = combine(*first)
    third = gate_up(2)
    sums_1 = combine(*second)
    hid_0 = hidden([sums_0])
    back_1 = back(edges[1], edges[3])
    sums_2 = combine(*third)
    deriv_0 = gather_rows(run, run_derivs(run, sums_0, back_0, 0, 0, share), place)
    dy_all = by_group(out_grad)
    xt_all = by_group(tokens).T
    hid_0_other = swap_dp(hid_0)
    down_grad = run_down_grad(run, hid_0, hid_0_other, dy_all, down_mask, place, 0, hidden_units, None)
    hid_1 = hidden([sums_1, sums_2])
    deriv_1 = gather_rows(run, run_derivs(run, sums_1, back_1, 0, 0, share), place)
    late = [
        gather_rows(run, run_derivs(run, sums_2, back_1, edges[2] - edges[1], t * rows, (t + 1) * rows), place)
        for t in range(pieces)
    ]
    deriv_0 = deriv_0()
    other_0 = swap_dp(deriv_0)
    grads = run_weight_grads(run, xt_all, [deriv_0], [other_0], masks, place, 0, hidden_units, None)
    hid_1_other = swap_dp(hid_1)
    keep, send = run_output(run, [hid_0, hid_1], down_weight, down_mask, place)
    output = col_scatter(keep, send, col)
    down_grad = run_down_grad(run, hid_1, hid_1_other, dy_all, down_mask, place, edges[1], hidden_units, down_grad)
    deriv_1 = deriv_1()
    other_1 = swap_dp(deriv_1)
    terms = run_token_terms(run, [deriv_0, deriv_1], gate_weight, up_weight, *masks, pieces)
    grads = run_weight_grads(run, xt_all, [deriv_1], [other_1], masks, place, edges[1], hidden_units, grads)
    token_grads, last, last_other = [], [], []
    for t in range(pieces):
        last.append(late[t]())
        last_other.append(swap_dp(last[t]))
        keep, send = run_token_grad(run, last[t], terms[t], gate_weight, up_weight, *masks, place, edges[2])
        token_grads.append(col_scatter(keep, send, col))
    grads = run_weight_grads(run, xt_all, last, last_other, masks, place, edges[2], hidden_units, grads)
    return output, cat(token_grads), *grads, down_grad


def plain_body(
    tokens, out_grad, gate_weight, up_weight, down_weight, gate_mask, up_mask, down_mask
):
    gate_keep = expand(gate_mask)
    up_keep = expand(up_mask)
    down_keep = expand(down_mask)
    gate_eff = gate_weight * gate_keep.astype(BF16)
    up_eff = up_weight * up_keep.astype(BF16)
    down_eff = down_weight * down_keep.astype(BF16)

    def scatter(array, axis):
        return lax.psum_scatter(array.astype(BF16), axis, scatter_dimension=0, tiled=True)

    def gather(array):
        return lax.all_gather(array, "row", axis=0, tiled=True)

    gate_share = scatter(dot(tokens, gate_eff), "row").astype(F32)
    up_share = scatter(dot(tokens, up_eff), "row").astype(F32)
    gate_sig = jax.nn.sigmoid(gate_share)
    silu_gate = gate_share * gate_sig
    hidden = gather((silu_gate * up_share).astype(BF16))
    output = scatter(dot(hidden, down_eff), "col")
    down_local = contract_rows(hidden, out_grad) * down_keep.astype(F32)
    back_share = scatter(contract_cols(out_grad, down_eff), "row").astype(F32)
    gate_deriv = back_share * up_share * gate_sig * (1.0 + gate_share * (1.0 - gate_sig))
    gate_full = gather(gate_deriv.astype(BF16))
    up_full = gather((back_share * silu_gate).astype(BF16))
    token_grad = scatter(contract_cols(gate_full, gate_eff) + contract_cols(up_full, up_eff), "col")
    gate_local = contract_rows(tokens, gate_full) * gate_keep.astype(F32)
    up_local = contract_rows(tokens, up_full) * up_keep.astype(F32)
    totals = [
        lax.psum(local.astype(BF16), "dp") for local in (gate_local, up_local, down_local)
    ]
    return (output, token_grad, *totals)


def solution(mesh):
    wide, tall = P("row", "col"), P("col", "row")
    tok, spread = P("dp", "row"), P(("dp", "col"), "row")
    body = plain_body
    if mesh.shape["row"] == 4 and mesh.shape["dp"] == 2 and mesh.shape["col"] == 4:
        body = fast_body
    return jax.shard_map(
        body,
        mesh=mesh,
        in_specs=(tok, tok, wide, wide, tall, wide, wide, tall),
        out_specs=(spread, spread, wide, wide, tall),
        check_vma=False,
    )
```

```python
import functools
import inspect

import jax
import jax.numpy as jnp
from jax import lax
from jax.experimental import pallas as pl
from jax.experimental.pallas import tpu as pltpu
from jax.sharding import PartitionSpec as P

BLOCK = 128
TILE = 512
F32 = jnp.float32
BF16 = jnp.bfloat16
ANY = pl.BlockSpec(memory_space=pl.ANY)
SMEM = pl.BlockSpec(memory_space=pltpu.SMEM)


def expand(mask_tile):
    return jnp.repeat(jnp.repeat(mask_tile, BLOCK, axis=0), BLOCK, axis=1)


def dot(left_side, right_side, left_dim=1, right_dim=0):
    return lax.dot_general(
        left_side, right_side, (((left_dim,), (right_dim,)), ((), ())), preferred_element_type=F32
    )


def contract_rows(left_side, right_side):
    return dot(left_side, right_side, 0, 0)


def contract_cols(left_side, right_side):
    return dot(left_side, right_side, 1, 1)


def pair_x(array):
    return lax.ppermute(array, "row", [(i, i ^ 1) for i in range(4)])


def pair_y(array):
    return lax.ppermute(array, "row", [(i, i ^ 2) for i in range(4)])


def pair_z(array, bit):
    return lax.ppermute(array, "col", [(i, i ^ bit) for i in range(4)])


def swap_dp(array):
    return lax.ppermute(array, "dp", [(0, 1), (1, 0)])


def cat(parts, axis=0):
    return lax.concatenate(parts, axis)


def shape_of(*dims):
    return jax.ShapeDtypeStruct(dims, BF16)


def full(array):
    return pl.BlockSpec(array.shape, lambda *at: (0,) * array.ndim)


class Runner:
    def __init__(self):
        self.last, self.count = None, 0
        self.waits, self.held = (), ()

    def after(self, *arrays):
        self.waits = arrays

    def hold(self, *arrays):
        self.holding = arrays

    holding = ()

    def __call__(self, kernel, grid, args, in_specs, out_shape, out_specs, scratch=(), flops=0, alias=None):
        name = "k%02d_%s" % (self.count, inspect.stack()[1].function[4:])
        self.count += 1
        single = not isinstance(out_shape, (tuple, list))
        out_shape = [out_shape] if single else list(out_shape)
        out_specs = [out_specs] if single else list(out_specs)
        last = [] if self.last is None else [self.last]
        holding = list(self.holding)
        extra = [*last, *self.waits, *holding]
        self.waits, self.holding = (), ()
        count, outs = len(args), len(out_shape)
        alias = dict(alias or {})
        for i in range(len(holding)):
            alias[count + len(extra) - len(holding) + i] = outs + i

        def wrapped(*refs):
            rest = refs[count + len(extra) :]
            kernel(*refs[:count], *rest[:outs], *rest[outs + len(holding) :])

        results = pl.pallas_call(
            wrapped,
            name=name,
            grid=grid,
            in_specs=list(in_specs) + [ANY] * len(extra),
            out_specs=out_specs + [ANY] * len(holding),
            out_shape=out_shape + [jax.ShapeDtypeStruct(a.shape, a.dtype) for a in holding],
            scratch_shapes=list(scratch),
            input_output_aliases=alias,
            compiler_params=pltpu.CompilerParams(vmem_limit_bytes=56 * 1024 * 1024),
            cost_estimate=pl.CostEstimate(flops=flops // (4 if 'terms' in name else 1), bytes_accessed=1 << 22, transcendentals=0),
        )(*args, *extra)
        self.last = results[0]
        self.held = tuple(results[outs:])
        return results[0] if single else results[:outs]


def masked(scr, weight_ref, mask_ref, row_at, col_at):
    rows, cols = weight_ref.shape
    for r in range(rows // BLOCK):
        for c in range(cols // BLOCK):
            at = (slice(r * BLOCK, (r + 1) * BLOCK), slice(c * BLOCK, (c + 1) * BLOCK))
            tile = weight_ref[at]
            scr[at] = jnp.where(mask_ref[row_at + r, col_at + c] > 0, tile, jnp.zeros_like(tile))
    return scr[...]


def store_masked(out_ref, row, grad, mask_ref, row_at, col_at):
    rows, cols = grad.shape
    for r in range(0, rows, BLOCK):
        for c in range(0, cols, BLOCK):
            tile = grad[r : r + BLOCK, c : c + BLOCK]
            kept = mask_ref[row_at + r // BLOCK, col_at + c // BLOCK] > 0
            out_ref[row + r : row + r + BLOCK, c : c + BLOCK] = jnp.where(kept, tile, jnp.zeros_like(tile))


def run_gate_up(run, tokens, gate_weight, up_weight, gate_mask, up_mask, place, lo, hi):
    count, width = tokens.shape
    n, base, share, cols = (hi - lo) // TILE, lo // TILE, count // 4, hi - lo

    def kernel(x_ref, wg_ref, wu_ref, mg_ref, mu_ref, place_ref, s0, s1, s2, g3, u3, w_scr, scr):
        part, j = pl.program_id(0), pl.program_id(1)

        def work(w_ref, m_ref, last):
            weight = masked(w_scr, w_ref, m_ref, 0, (base + j) * (TILE // BLOCK))
            scr[...] = dot(x_ref[...], weight).astype(BF16)
            for k, out in enumerate((s0, s1, s2, last)):
                out[...] = scr[pl.ds(pl.multiple_of((place_ref[0] ^ k) * share, share), share), :]

        pl.when(part == 0)(lambda: work(wg_ref, mg_ref, g3))
        pl.when(part == 1)(lambda: work(wu_ref, mu_ref, u3))

    def first(p, j):
        return (0, jnp.where(p == 0, j, n - 1))

    def second(p, j):
        return (0, jnp.where(p == 0, 0, j))

    both = pl.BlockSpec((share, TILE), lambda p, j: (0, p * n + j))
    return run(
        kernel,
        (2, n),
        (tokens, gate_weight, up_weight, gate_mask, up_mask, place),
        [
            full(tokens),
            pl.BlockSpec((width, TILE), lambda p, j: (0, base + jnp.where(p == 0, j, n - 1))),
            pl.BlockSpec((width, TILE), lambda p, j: (0, base + jnp.where(p == 0, 0, j))),
            SMEM,
            SMEM,
            SMEM,
        ],
        [shape_of(share, 2 * cols)] * 3 + [shape_of(share, cols)] * 2,
        [both] * 3 + [pl.BlockSpec((share, TILE), first), pl.BlockSpec((share, TILE), second)],
        [pltpu.VMEM((width, TILE), BF16), pltpu.VMEM((count, TILE), BF16)],
        flops=4 * count * width * cols,
    )


def run_combine(run, one, two, got_gate, got_up):
    share, cols = got_up.shape

    def kernel(one_ref, two_ref, gate_ref, up_ref, one_out, two_out):
        one_out[...] = (one_ref[...].astype(F32) + up_ref[...].astype(F32)).astype(BF16)
        two_out[...] = (two_ref[...].astype(F32) + gate_ref[...].astype(F32)).astype(BF16)

    rows = share // 2
    low = pl.BlockSpec((rows, cols), lambda j: (j, 0))
    high = pl.BlockSpec((rows, cols), lambda j: (j, 1))
    return run(
        kernel,
        (2,),
        (one, two, got_gate, got_up),
        [high, low, low, low],
        [shape_of(*one.shape)] * 2,
        [high, low],
        alias={0: 0, 1: 1},
    )


def run_back(run, out_grad, down_weight, down_mask):
    count, width = out_grad.shape
    hidden_units = down_weight.shape[0]

    def kernel(dy_ref, wd_ref, md_ref, out_ref, w_scr):
        weight = masked(w_scr, wd_ref, md_ref, pl.program_id(0) * (TILE // BLOCK), 0)
        out_ref[...] = dot(dy_ref[...], weight, 1, 1).astype(BF16)

    return run(
        kernel,
        (hidden_units // TILE,),
        (out_grad, down_weight, down_mask),
        [full(out_grad), pl.BlockSpec((TILE, width), lambda j: (j, 0)), SMEM],
        shape_of(count, hidden_units),
        pl.BlockSpec((count, TILE), lambda j: (0, j)),
        [pltpu.VMEM((TILE, width), BF16)],
        flops=2 * count * width * hidden_units,
    )


def add_three(refs, col, width):
    first, second, third = (ref[:, col : col + width].astype(F32) for ref in refs)
    return first + second + third


STEP = 256


def run_hidden(run, sums):
    share = sums[0][0].shape[0]
    widths = [group[0].shape[1] // 2 for group in sums]
    rows = share // 6

    def kernel(*refs):
        out_ref, start = refs[-1], 0
        for i, cols in enumerate(widths):
            group = refs[3 * i : 3 * i + 3]
            for at in range(0, cols, STEP):
                gate, up = add_three(group, at, STEP), add_three(group, cols + at, STEP)
                out_ref[:, start + at : start + at + STEP] = (gate * jax.nn.sigmoid(gate) * up).astype(BF16)
            start += cols

    flat = [array for group in sums for array in group]
    return run(
        kernel,
        (share // rows,),
        flat,
        [pl.BlockSpec((rows, array.shape[1]), lambda j: (j, 0)) for array in flat],
        shape_of(share, sum(widths)),
        pl.BlockSpec((rows, sum(widths)), lambda j: (j, 0)),
    )


def run_derivs(run, sums, back, back_at, row_lo, row_hi):
    cols = sums[0].shape[1] // 2
    rows = 32
    base = row_lo // rows

    def kernel(s0, s1, s2, back_ref, out_ref):
        for at in range(0, cols, STEP):
            gate, up = add_three((s0, s1, s2), at, STEP), add_three((s0, s1, s2), cols + at, STEP)
            grad = back_ref[:, at : at + STEP].astype(F32)
            sig = jax.nn.sigmoid(gate)
            silu = gate * sig
            out_ref[:, at : at + STEP] = (grad * up * (sig + silu * (1.0 - sig))).astype(BF16)
            out_ref[:, cols + at : cols + at + STEP] = (grad * silu).astype(BF16)

    return run(
        kernel,
        ((row_hi - row_lo) // rows,),
        (*sums, back),
        [pl.BlockSpec((rows, 2 * cols), lambda j: (base + j, 0))] * 3
        + [pl.BlockSpec((pl.Element(rows), pl.Element(cols)), lambda j: ((base + j) * rows, back_at))],
        shape_of(row_hi - row_lo, 2 * cols),
        pl.BlockSpec((rows, 2 * cols), lambda j: (j, 0)),
    )


def run_assemble(run, parts, place):
    rows, width = parts[0].shape
    half = rows // 2

    def kernel(*refs):
        place_ref, out_ref = refs[5], refs[6]
        for k, part in enumerate(refs[:5]):
            at = (place_ref[0] ^ min(k, 3)) * rows + (half if k == 4 else 0)
            out_ref[pl.ds(pl.multiple_of(at, half), part.shape[0]), :] = part[...]

    return run(
        kernel,
        (width // TILE,),
        (*parts, place),
        [pl.BlockSpec((part.shape[0], TILE), lambda j: (0, j)) for part in parts] + [SMEM],
        shape_of(4 * rows, width),
        pl.BlockSpec((4 * rows, TILE), lambda j: (0, j)),
    )


def gather_far(run, own, got, place):
    half = own.shape[0] // 2
    far = [pair_y(got[0][:half]), pair_x(got[1][half:])]
    return lambda: run_assemble(run, (own, *got, *far), place)


def write_col_halves(total, place_ref, keep_ref, send_ref, scr):
    rows = total.shape[0] // 4
    scr[...] = total.astype(BF16)
    low = place_ref[2] & 1
    for i in range(2):
        keep_ref[i * rows : (i + 1) * rows] = scr[pl.ds(pl.multiple_of((2 * i + low) * rows, rows), rows), :]
        send_ref[i * rows : (i + 1) * rows] = scr[pl.ds(pl.multiple_of((2 * i + 1 - low) * rows, rows), rows), :]


def col_halves(count, width):
    spec = pl.BlockSpec((count // 2, TILE), lambda j: (0, j))
    return [shape_of(count // 2, width)] * 2, [spec] * 2, [pltpu.VMEM((count, TILE), BF16)]


def run_col_first(run, keep, got, place):
    rows, width = keep.shape[0] // 2, keep.shape[1]

    def kernel(keep_ref, got_ref, place_ref, keep_out, send_out, scr):
        scr[...] = (keep_ref[...].astype(F32) + got_ref[...].astype(F32)).astype(BF16)
        high = place_ref[2] // 2
        keep_out[...] = scr[pl.ds(pl.multiple_of(high * rows, rows), rows), :]
        send_out[...] = scr[pl.ds(pl.multiple_of((1 - high) * rows, rows), rows), :]

    whole = pl.BlockSpec((2 * rows, TILE), lambda j: (0, j))
    return run(
        kernel,
        (width // TILE,),
        (keep, got, place),
        [whole, whole, SMEM],
        [shape_of(rows, width)] * 2,
        [pl.BlockSpec((rows, TILE), lambda j: (0, j))] * 2,
        [pltpu.VMEM((2 * rows, TILE), BF16)],
    )


def run_col_second(run, pairs):
    sizes = [keep.shape[0] for keep, _ in pairs]
    width = pairs[0][0].shape[1]
    flat = [array for pair in pairs for array in pair]

    def kernel(*refs):
        start = 0
        for t, rows in enumerate(sizes):
            total = refs[2 * t][...].astype(F32) + refs[2 * t + 1][...].astype(F32)
            refs[-1][start : start + rows] = total.astype(BF16)
            start += rows

    return run(
        kernel,
        (width // TILE,),
        flat,
        [pl.BlockSpec((array.shape[0], TILE), lambda j: (0, j)) for array in flat],
        shape_of(sum(sizes), width),
        pl.BlockSpec((sum(sizes), TILE), lambda j: (0, j)),
    )


def run_fence(run, *arrays):
    def kernel(out_ref):
        out_ref[...] = jnp.zeros_like(out_ref)

    run.hold(*arrays)
    run(kernel, (), (), [], shape_of(16, BLOCK), pl.BlockSpec((16, BLOCK), lambda: (0, 0)))
    return run.held


def run_by_group(run, tokens, tokens_other, dy, dy_other, place):
    count, width = tokens.shape
    step = 256

    def kernel(x_ref, xo_ref, dy_ref, dyo_ref, place_ref, xt_out, dy_out):
        for x, y, group in ((x_ref, dy_ref, place_ref[1]), (xo_ref, dyo_ref, 1 - place_ref[1])):
            at = pl.ds(pl.multiple_of(group * count, count), count)
            xt_out[:, at] = x[...].T
            dy_out[at, :] = y[...]

    return run(
        kernel,
        (width // step,),
        (tokens, tokens_other, dy, dy_other, place),
        [pl.BlockSpec((count, step), lambda j: (0, j))] * 4 + [SMEM],
        [shape_of(width, 2 * count), shape_of(2 * count, width)],
        [pl.BlockSpec((step, 2 * count), lambda j: (j, 0)), pl.BlockSpec((2 * count, step), lambda j: (0, j))],
    )


def run_output(run, hiddens, down_weight, down_mask, place):
    count = hiddens[0].shape[0]
    hidden_units, width = down_weight.shape

    def kernel(*refs):
        h_refs = refs[: len(hiddens)]
        wd_ref, md_ref, place_ref, keep_ref, send_ref, scr, w_scr = refs[len(hiddens) :]
        weight = masked(w_scr, wd_ref, md_ref, 0, pl.program_id(0) * (TILE // BLOCK))
        total, at = None, 0
        for h_ref in h_refs:
            cols = h_ref.shape[1]
            term = dot(h_ref[...], weight[at : at + cols])
            total, at = term if total is None else total + term, at + cols
        write_col_halves(total, place_ref, keep_ref, send_ref, scr)

    shapes, specs, scratch = col_halves(count, width)
    return run(
        kernel,
        (width // TILE,),
        (*hiddens, down_weight, down_mask, place),
        [full(h) for h in hiddens] + [pl.BlockSpec((hidden_units, TILE), lambda j: (0, j)), SMEM, SMEM],
        shapes,
        specs,
        scratch + [pltpu.VMEM((hidden_units, TILE), BF16)],
        flops=2 * count * hidden_units * width,
    )


def weight_blocks(derivs, starts):
    return [lo // TILE + q for d, lo in zip(derivs, starts) for q in range(d.shape[1] // 2 // TILE)]


def run_token_terms(run, derivs, starts, gate_weight, up_weight, gate_mask, up_mask):
    count, width = derivs[0].shape[0], gate_weight.shape[0]
    blocks = weight_blocks(derivs, starts)
    n = len(blocks)

    def kernel(*refs):
        d_refs, weights = refs[: len(derivs)], refs[len(derivs) : len(derivs) + 2 * n]
        mg_ref, mu_ref, out_ref, w_scr = refs[len(derivs) + 2 * n :]
        row_at = pl.program_id(0) * (TILE // BLOCK)
        total, i = None, 0
        for d_ref in d_refs:
            steps = d_ref.shape[1] // 2 // TILE
            for q in range(steps):
                for part, m_ref in ((0, mg_ref), (1, mu_ref)):
                    at = part * n + i
                    weight = masked(w_scr.at[at], weights[at], m_ref, row_at, blocks[i] * (TILE // BLOCK))
                    start = (part * steps + q) * TILE
                    term = dot(d_ref[:, start : start + TILE], weight, 1, 1)
                    total = term if total is None else total + term
                i += 1
        out_ref[...] = total

    weight_specs = [pl.BlockSpec((TILE, TILE), functools.partial(lambda q, j: (j, q), q)) for q in blocks]
    return run(
        kernel,
        (width // TILE,),
        (*derivs, *[gate_weight] * n, *[up_weight] * n, gate_mask, up_mask),
        [full(d) for d in derivs] + weight_specs * 2 + [SMEM] * 2,
        jax.ShapeDtypeStruct((count, width), F32),
        pl.BlockSpec((count, TILE), lambda j: (0, j)),
        [pltpu.VMEM((2 * n, TILE, TILE), BF16)],
        flops=4 * count * n * TILE * width,
    )


def run_token_grad(run, deriv, terms, gate_weight, up_weight, gate_mask, up_mask, place, lo, t, pieces):
    count, width = terms.shape
    share = count // 4
    rows = share // pieces
    blocks = weight_blocks([deriv], [lo])
    n = len(blocks)

    def kernel(*refs):
        d_ref, terms_ref = refs[:2]
        mg_ref, mu_ref, place_ref, keep_ref, send_ref, scr, w_scr, d_scr = refs[2 + 2 * n :]
        j = pl.program_id(0)

        def gather():
            for owner in range(4):
                start = owner * share + t * rows
                d_scr[owner * rows : (owner + 1) * rows] = d_ref[start : start + rows]

        pl.when(j == 0)(gather)
        total = None
        for i in range(2 * n):
            m_ref = mg_ref if i < n else mu_ref
            weight = masked(
                w_scr.at[i], refs[2 + i], m_ref, j * (TILE // BLOCK), blocks[i % n] * (TILE // BLOCK)
            )
            term = dot(d_scr[:, i * TILE : (i + 1) * TILE], weight, 1, 1)
            total = term if total is None else total + term
        low = place_ref[2] & 1
        for owner in range(4):
            start = owner * share + t * rows
            scr[owner * rows : (owner + 1) * rows] = (
                total[owner * rows : (owner + 1) * rows] + terms_ref[start : start + rows]
            ).astype(BF16)
        for i in range(2):
            for ref, bit in ((keep_ref, low), (send_ref, 1 - low)):
                ref[i * rows : (i + 1) * rows] = scr[pl.ds(pl.multiple_of((2 * i + bit) * rows, rows), rows), :]

    shapes, specs, scratch = col_halves(4 * rows, width)
    weight_specs = [pl.BlockSpec((TILE, TILE), functools.partial(lambda q, j: (j, q), q)) for q in blocks]
    return run(
        kernel,
        (width // TILE,),
        (deriv, terms, *[gate_weight] * n, *[up_weight] * n, gate_mask, up_mask, place),
        [full(deriv), pl.BlockSpec((count, TILE), lambda j: (0, j))] + weight_specs * 2 + [SMEM] * 3,
        shapes,
        specs,
        scratch + [pltpu.VMEM((2 * n, TILE, TILE), BF16), pltpu.VMEM((4 * rows, deriv.shape[1]), BF16)],
        flops=16 * rows * n * TILE * width,
    )


def both_groups(dst, own, other, place_ref, count):
    for ref, group in ((own, place_ref[1]), (other, 1 - place_ref[1])):
        dst[pl.ds(pl.multiple_of(group * count, count), count), :] = ref[...]


def run_down_grad(run, hid, hid_other, dy_all, down_mask, place, lo, hidden_units, so_far):
    count, cols = hid.shape
    width = dy_all.shape[1]
    n, base = cols // TILE, lo // TILE
    more = [] if so_far is None else [so_far]

    def kernel(*refs):
        h_ref, ho_ref, dy_ref, md_ref, place_ref = refs[:5]
        out_ref, h_all = refs[-2:]
        j = pl.program_id(0)
        both_groups(h_all, h_ref, ho_ref, place_ref, count)
        left = h_all[...]
        for at in range(0, width, 512):
            grad = dot(left, dy_ref[:, at : at + 512], 0, 0).astype(BF16)
            store_masked(out_ref.at[:, at : at + 512], 0, grad, md_ref, (base + j) * (TILE // BLOCK), at // BLOCK)

    return run(
        kernel,
        (n,),
        (hid, hid_other, dy_all, down_mask, place, *more),
        [pl.BlockSpec((count, TILE), lambda j: (0, j))] * 2 + [full(dy_all), SMEM, SMEM] + [ANY] * len(more),
        shape_of(hidden_units, width),
        pl.BlockSpec((TILE, width), lambda j: (base + j, 0)),
        [pltpu.VMEM((2 * count, TILE), BF16)],
        flops=4 * count * width * cols,
        alias={5: 0} if more else None,
    )


def run_weight_grads(run, xt_all, deriv, deriv_other, masks, place, lo, hidden_units, so_far):
    width, all_count = xt_all.shape
    count = all_count // 2
    cols = deriv.shape[1] // 2
    n, base = cols // TILE, lo // TILE
    more = [] if so_far is None else list(so_far)

    def kernel(xt_ref, dg, du, dgo, duo, mg_ref, mu_ref, place_ref, *rest):
        gate_out, up_out, d_all = rest[-3:]
        col_at = (base + pl.program_id(0)) * (TILE // BLOCK)
        for own, other, m_ref, out in ((dg, dgo, mg_ref, gate_out), (du, duo, mu_ref, up_out)):
            both_groups(d_all, own, other, place_ref, count)
            right = d_all[...]
            for at in range(0, width, 512):
                grad = dot(xt_ref[at : at + 512], right).astype(BF16)
                store_masked(out, at, grad, m_ref, at // BLOCK, col_at)

    gate_spec = pl.BlockSpec((count, TILE), lambda j: (0, j))
    up_spec = pl.BlockSpec((count, TILE), lambda j: (0, n + j))
    return run(
        kernel,
        (n,),
        (xt_all, deriv, deriv, deriv_other, deriv_other, *masks, place, *more),
        [full(xt_all)] + [gate_spec, up_spec] * 2 + [SMEM] * 3 + [ANY] * len(more),
        [shape_of(width, hidden_units)] * 2,
        [pl.BlockSpec((width, TILE), lambda j: (0, base + j))] * 2,
        [pltpu.VMEM((all_count, TILE), BF16)],
        flops=8 * count * width * cols,
        alias={8: 0, 9: 1} if more else None,
    )


def fast_body(tokens, out_grad, gate_weight, up_weight, down_weight, gate_mask, up_mask, down_mask):
    run = Runner()
    row, dp, col = (lax.axis_index(name) for name in ("row", "dp", "col"))
    place = jnp.stack([row, dp, col]).astype(jnp.int32)
    count, width = tokens.shape
    share = count // 4
    hidden_units = gate_weight.shape[1]
    masks = (gate_mask, up_mask)
    tiles = hidden_units // TILE
    edges = [0, tiles * 2 // 7 * TILE, tiles * 5 // 7 * TILE, hidden_units]
    pieces = 2
    rows = share // pieces

    def gate_up(i):
        parts = run_gate_up(run, tokens, gate_weight, up_weight, *masks, place, edges[i], edges[i + 1])
        return parts, pair_x(parts[3]), pair_y(parts[4])

    def combine(parts, got_gate, got_up):
        one, two = run_combine(run, parts[1], parts[2], got_gate, got_up)
        return parts[0], pair_x(one), pair_y(two)

    def gather(array):
        return lax.all_gather(array, "row", axis=0, tiled=True)

    def derivs(sums, i):
        return run_derivs(run, sums, back, edges[i], 0, share)

    def down(hid, other, i, so_far):
        return run_down_grad(run, hid, other, dy_all, down_mask, place, edges[i], hidden_units, so_far)

    def weights(deriv, other, i, so_far):
        return run_weight_grads(run, xt_all, deriv, other, masks, place, edges[i], hidden_units, so_far)

    tokens_other, dy_other = swap_dp(tokens), swap_dp(out_grad)
    back = run_back(run, out_grad, down_weight, down_mask)
    back = lax.psum_scatter(back, "row", scatter_dimension=0, tiled=True)
    first = gate_up(0)
    run.after(tokens_other, dy_other)
    second = gate_up(1)
    sums_0 = combine(*first)
    third = gate_up(2)
    sums_1 = combine(*second)
    xt_all, dy_all = run_by_group(run, tokens, tokens_other, out_grad, dy_other, place)
    sums_2 = combine(*third)
    run.after(back)
    hid_0 = gather(run_hidden(run, [sums_0, sums_1]))
    own_1 = derivs(sums_1, 1)
    near_1 = pair_x(own_1), pair_y(own_1)
    deriv_0 = derivs(sums_0, 0)
    hid_2 = run_hidden(run, [sums_2])
    run.hold(hid_0, hid_2)
    deriv_2 = derivs(sums_2, 2)
    hid_0, hid_2 = run.held
    hid_2 = gather(hid_2)
    hid_0_other = swap_dp(hid_0)
    down_grad = down(hid_0, hid_0_other, 0, None)
    *near_1, hid_2, deriv_0 = run_fence(run, *near_1, hid_2, deriv_0)
    deriv_1 = gather_far(run, own_1, near_1, place)
    deriv_0 = gather(deriv_0)
    out_keep, send = run_output(run, [hid_0, hid_2], down_weight, down_mask, place)
    out_got = pair_z(send, 1)
    deriv_1 = deriv_1()
    grads = weights(deriv_1, swap_dp(deriv_1), 1, None)
    run.after(out_got)
    deriv_0, deriv_2, hid_2 = run_fence(run, deriv_0, deriv_2, hid_2)
    deriv_2 = gather(deriv_2)
    out_keep, send = run_col_first(run, out_keep, out_got, place)
    out_got = pair_z(send, 2)
    grads = weights(deriv_0, swap_dp(deriv_0), 0, grads)
    terms = run_token_terms(run, [deriv_0, deriv_1], [0, edges[1]], gate_weight, up_weight, *masks)
    run.after(out_got)
    (deriv_2,) = run_fence(run, deriv_2)
    halves = []
    for t in range(pieces):
        keep, send = run_token_grad(
            run, deriv_2, terms, gate_weight, up_weight, *masks, place, edges[2], t, pieces
        )
        halves.append((keep, pair_z(send, 1)))
    grads = weights(deriv_2, swap_dp(deriv_2), 2, grads)
    pairs = []
    for keep, got in halves:
        keep, send = run_col_first(run, keep, got, place)
        pairs.append((keep, pair_z(send, 2)))
    down_grad = down(hid_2, swap_dp(hid_2), 2, down_grad)
    output = run_col_second(run, [(out_keep, out_got)])
    token_grad = run_col_second(run, pairs)
    return output, token_grad, *grads, down_grad


def plain_body(
    tokens, out_grad, gate_weight, up_weight, down_weight, gate_mask, up_mask, down_mask
):
    gate_keep = expand(gate_mask)
    up_keep = expand(up_mask)
    down_keep = expand(down_mask)
    gate_eff = gate_weight * gate_keep.astype(BF16)
    up_eff = up_weight * up_keep.astype(BF16)
    down_eff = down_weight * down_keep.astype(BF16)

    def scatter(array, axis):
        return lax.psum_scatter(array.astype(BF16), axis, scatter_dimension=0, tiled=True)

    def gather(array):
        return lax.all_gather(array, "row", axis=0, tiled=True)

    gate_share = scatter(dot(tokens, gate_eff), "row").astype(F32)
    up_share = scatter(dot(tokens, up_eff), "row").astype(F32)
    gate_sig = jax.nn.sigmoid(gate_share)
    silu_gate = gate_share * gate_sig
    hidden = gather((silu_gate * up_share).astype(BF16))
    output = scatter(dot(hidden, down_eff), "col")
    down_local = contract_rows(hidden, out_grad) * down_keep.astype(F32)
    back_share = scatter(contract_cols(out_grad, down_eff), "row").astype(F32)
    gate_deriv = back_share * up_share * gate_sig * (1.0 + gate_share * (1.0 - gate_sig))
    gate_full = gather(gate_deriv.astype(BF16))
    up_full = gather((back_share * silu_gate).astype(BF16))
    token_grad = scatter(contract_cols(gate_full, gate_eff) + contract_cols(up_full, up_eff), "col")
    gate_local = contract_rows(tokens, gate_full) * gate_keep.astype(F32)
    up_local = contract_rows(tokens, up_full) * up_keep.astype(F32)
    totals = [
        lax.psum(local.astype(BF16), "dp") for local in (gate_local, up_local, down_local)
    ]
    return (output, token_grad, *totals)


def solution(mesh):
    wide, tall = P("row", "col"), P("col", "row")
    tok, spread = P("dp", "row"), P(("dp", "col"), "row")
    body = plain_body
    if mesh.shape["row"] == 4 and mesh.shape["dp"] == 2 and mesh.shape["col"] == 4:
        body = fast_body
    return jax.shard_map(
        body,
        mesh=mesh,
        in_specs=(tok, tok, wide, wide, tall, wide, wide, tall),
        out_specs=(spread, spread, wide, wide, tall),
        check_vma=False,
    )
```

```python
import functools
import inspect

import jax
import jax.numpy as jnp
from jax import lax
from jax.experimental import pallas as pl
from jax.experimental.pallas import tpu as pltpu
from jax.sharding import PartitionSpec as P

BLOCK = 128
TILE = 512
F32 = jnp.float32
BF16 = jnp.bfloat16
ANY = pl.BlockSpec(memory_space=pl.ANY)
SMEM = pl.BlockSpec(memory_space=pltpu.SMEM)


def expand(mask_tile):
    return jnp.repeat(jnp.repeat(mask_tile, BLOCK, axis=0), BLOCK, axis=1)


def dot(left_side, right_side, left_dim=1, right_dim=0):
    return lax.dot_general(
        left_side, right_side, (((left_dim,), (right_dim,)), ((), ())), preferred_element_type=F32
    )


def contract_rows(left_side, right_side):
    return dot(left_side, right_side, 0, 0)


def contract_cols(left_side, right_side):
    return dot(left_side, right_side, 1, 1)


def pair_x(array):
    return lax.ppermute(array, "row", [(i, i ^ 1) for i in range(4)])


def pair_y(array):
    return lax.ppermute(array, "row", [(i, i ^ 2) for i in range(4)])


def pair_z(array, bit):
    return lax.ppermute(array, "col", [(i, i ^ bit) for i in range(4)])


def swap_dp(array):
    return lax.ppermute(array, "dp", [(0, 1), (1, 0)])


def cat(parts, axis=0):
    return lax.concatenate(parts, axis)


def shape_of(*dims):
    return jax.ShapeDtypeStruct(dims, BF16)


def full(array):
    return pl.BlockSpec(array.shape, lambda *at: (0,) * array.ndim)


class Runner:
    def __init__(self):
        self.last, self.count = None, 0
        self.waits, self.held = (), ()

    def after(self, *arrays):
        self.waits = arrays

    def hold(self, *arrays):
        self.holding = arrays

    holding = ()

    def __call__(self, kernel, grid, args, in_specs, out_shape, out_specs, scratch=(), flops=0, alias=None):
        name = "k%02d_%s" % (self.count, inspect.stack()[1].function[4:])
        self.count += 1
        single = not isinstance(out_shape, (tuple, list))
        out_shape = [out_shape] if single else list(out_shape)
        out_specs = [out_specs] if single else list(out_specs)
        last = [] if self.last is None else [self.last]
        holding = list(self.holding)
        extra = [*last, *self.waits, *holding]
        self.waits, self.holding = (), ()
        count, outs = len(args), len(out_shape)
        alias = dict(alias or {})
        for i in range(len(holding)):
            alias[count + len(extra) - len(holding) + i] = outs + i

        def wrapped(*refs):
            rest = refs[count + len(extra) :]
            kernel(*refs[:count], *rest[:outs], *rest[outs + len(holding) :])

        results = pl.pallas_call(
            wrapped,
            name=name,
            grid=grid,
            in_specs=list(in_specs) + [ANY] * len(extra),
            out_specs=out_specs + [ANY] * len(holding),
            out_shape=out_shape + [jax.ShapeDtypeStruct(a.shape, a.dtype) for a in holding],
            scratch_shapes=list(scratch),
            input_output_aliases=alias,
            compiler_params=pltpu.CompilerParams(vmem_limit_bytes=56 * 1024 * 1024),
            cost_estimate=pl.CostEstimate(flops=flops // (4 if 'terms' in name else 1), bytes_accessed=1 << 22, transcendentals=0),
        )(*args, *extra)
        self.last = results[0]
        self.held = tuple(results[outs:])
        return results[0] if single else results[:outs]


def masked(scr, weight_ref, mask_ref, row_at, col_at):
    rows, cols = weight_ref.shape
    for r in range(rows // BLOCK):
        for c in range(cols // BLOCK):
            at = (slice(r * BLOCK, (r + 1) * BLOCK), slice(c * BLOCK, (c + 1) * BLOCK))
            tile = weight_ref[at]
            scr[at] = jnp.where(mask_ref[row_at + r, col_at + c] > 0, tile, jnp.zeros_like(tile))
    return scr[...]


def store_masked(out_ref, row, grad, mask_ref, row_at, col_at):
    rows, cols = grad.shape
    for r in range(0, rows, BLOCK):
        for c in range(0, cols, BLOCK):
            tile = grad[r : r + BLOCK, c : c + BLOCK]
            kept = mask_ref[row_at + r // BLOCK, col_at + c // BLOCK] > 0
            out_ref[row + r : row + r + BLOCK, c : c + BLOCK] = jnp.where(kept, tile, jnp.zeros_like(tile))


def run_gate_up(run, tokens, gate_weight, up_weight, gate_mask, up_mask, place, lo, hi):
    count, width = tokens.shape
    n, base, share, cols = (hi - lo) // TILE, lo // TILE, count // 4, hi - lo

    def kernel(x_ref, wg_ref, wu_ref, mg_ref, mu_ref, place_ref, s0, s1, s2, g3, u3, w_scr, scr):
        part, j = pl.program_id(0), pl.program_id(1)

        def work(w_ref, m_ref, last):
            weight = masked(w_scr, w_ref, m_ref, 0, (base + j) * (TILE // BLOCK))
            scr[...] = dot(x_ref[...], weight).astype(BF16)
            for k, out in enumerate((s0, s1, s2, last)):
                out[...] = scr[pl.ds(pl.multiple_of((place_ref[0] ^ k) * share, share), share), :]

        pl.when(part == 0)(lambda: work(wg_ref, mg_ref, g3))
        pl.when(part == 1)(lambda: work(wu_ref, mu_ref, u3))

    def first(p, j):
        return (0, jnp.where(p == 0, j, n - 1))

    def second(p, j):
        return (0, jnp.where(p == 0, 0, j))

    both = pl.BlockSpec((share, TILE), lambda p, j: (0, p * n + j))
    return run(
        kernel,
        (2, n),
        (tokens, gate_weight, up_weight, gate_mask, up_mask, place),
        [
            full(tokens),
            pl.BlockSpec((width, TILE), lambda p, j: (0, base + jnp.where(p == 0, j, n - 1))),
            pl.BlockSpec((width, TILE), lambda p, j: (0, base + jnp.where(p == 0, 0, j))),
            SMEM,
            SMEM,
            SMEM,
        ],
        [shape_of(share, 2 * cols)] * 3 + [shape_of(share, cols)] * 2,
        [both] * 3 + [pl.BlockSpec((share, TILE), first), pl.BlockSpec((share, TILE), second)],
        [pltpu.VMEM((width, TILE), BF16), pltpu.VMEM((count, TILE), BF16)],
        flops=4 * count * width * cols,
    )


def run_combine(run, one, two, got_gate, got_up):
    share, cols = got_up.shape

    def kernel(one_ref, two_ref, gate_ref, up_ref, one_out, two_out):
        one_out[...] = (one_ref[...].astype(F32) + up_ref[...].astype(F32)).astype(BF16)
        two_out[...] = (two_ref[...].astype(F32) + gate_ref[...].astype(F32)).astype(BF16)

    rows = share // 2
    low = pl.BlockSpec((rows, cols), lambda j: (j, 0))
    high = pl.BlockSpec((rows, cols), lambda j: (j, 1))
    return run(
        kernel,
        (2,),
        (one, two, got_gate, got_up),
        [high, low, low, low],
        [shape_of(*one.shape)] * 2,
        [high, low],
        alias={0: 0, 1: 1},
    )


def run_back(run, out_grad, down_weight, down_mask):
    count, width = out_grad.shape
    hidden_units = down_weight.shape[0]

    def kernel(dy_ref, wd_ref, md_ref, out_ref, w_scr):
        weight = masked(w_scr, wd_ref, md_ref, pl.program_id(0) * (TILE // BLOCK), 0)
        out_ref[...] = dot(dy_ref[...], weight, 1, 1).astype(BF16)

    return run(
        kernel,
        (hidden_units // TILE,),
        (out_grad, down_weight, down_mask),
        [full(out_grad), pl.BlockSpec((TILE, width), lambda j: (j, 0)), SMEM],
        shape_of(count, hidden_units),
        pl.BlockSpec((count, TILE), lambda j: (0, j)),
        [pltpu.VMEM((TILE, width), BF16)],
        flops=2 * count * width * hidden_units,
    )


def add_three(refs, col, width):
    first, second, third = (ref[:, col : col + width].astype(F32) for ref in refs)
    return first + second + third


STEP = 256


def run_hidden(run, sums):
    share = sums[0][0].shape[0]
    widths = [group[0].shape[1] // 2 for group in sums]
    rows = share // 6

    def kernel(*refs):
        out_ref, start = refs[-1], 0
        for i, cols in enumerate(widths):
            group = refs[3 * i : 3 * i + 3]
            for at in range(0, cols, STEP):
                gate, up = add_three(group, at, STEP), add_three(group, cols + at, STEP)
                out_ref[:, start + at : start + at + STEP] = (gate * jax.nn.sigmoid(gate) * up).astype(BF16)
            start += cols

    flat = [array for group in sums for array in group]
    return run(
        kernel,
        (share // rows,),
        flat,
        [pl.BlockSpec((rows, array.shape[1]), lambda j: (j, 0)) for array in flat],
        shape_of(share, sum(widths)),
        pl.BlockSpec((rows, sum(widths)), lambda j: (j, 0)),
    )


def run_derivs(run, sums, back, back_at, row_lo, row_hi):
    cols = sums[0].shape[1] // 2
    rows = 32
    base = row_lo // rows

    def kernel(s0, s1, s2, back_ref, out_ref):
        for at in range(0, cols, STEP):
            gate, up = add_three((s0, s1, s2), at, STEP), add_three((s0, s1, s2), cols + at, STEP)
            grad = back_ref[:, at : at + STEP].astype(F32)
            sig = jax.nn.sigmoid(gate)
            silu = gate * sig
            out_ref[:, at : at + STEP] = (grad * up * (sig + silu * (1.0 - sig))).astype(BF16)
            out_ref[:, cols + at : cols + at + STEP] = (grad * silu).astype(BF16)

    return run(
        kernel,
        ((row_hi - row_lo) // rows,),
        (*sums, back),
        [pl.BlockSpec((rows, 2 * cols), lambda j: (base + j, 0))] * 3
        + [pl.BlockSpec((pl.Element(rows), pl.Element(cols)), lambda j: ((base + j) * rows, back_at))],
        shape_of(row_hi - row_lo, 2 * cols),
        pl.BlockSpec((rows, 2 * cols), lambda j: (j, 0)),
    )


def run_assemble(run, parts, place):
    rows, width = parts[0].shape
    half = rows // 2

    def kernel(*refs):
        place_ref, out_ref = refs[5], refs[6]
        for k, part in enumerate(refs[:5]):
            at = (place_ref[0] ^ min(k, 3)) * rows + (half if k == 4 else 0)
            out_ref[pl.ds(pl.multiple_of(at, half), part.shape[0]), :] = part[...]

    return run(
        kernel,
        (width // TILE,),
        (*parts, place),
        [pl.BlockSpec((part.shape[0], TILE), lambda j: (0, j)) for part in parts] + [SMEM],
        shape_of(4 * rows, width),
        pl.BlockSpec((4 * rows, TILE), lambda j: (0, j)),
    )


def gather_far(run, own, got, place):
    half = own.shape[0] // 2
    far = [pair_y(got[0][:half]), pair_x(got[1][half:])]
    return lambda: run_assemble(run, (own, *got, *far), place)


def write_col_halves(total, place_ref, keep_ref, send_ref, scr):
    rows = total.shape[0] // 4
    scr[...] = total.astype(BF16)
    low = place_ref[2] & 1
    for i in range(2):
        keep_ref[i * rows : (i + 1) * rows] = scr[pl.ds(pl.multiple_of((2 * i + low) * rows, rows), rows), :]
        send_ref[i * rows : (i + 1) * rows] = scr[pl.ds(pl.multiple_of((2 * i + 1 - low) * rows, rows), rows), :]


def col_halves(count, width):
    spec = pl.BlockSpec((count // 2, TILE), lambda j: (0, j))
    return [shape_of(count // 2, width)] * 2, [spec] * 2, [pltpu.VMEM((count, TILE), BF16)]


def run_col_first(run, keep, got, place):
    rows, width = keep.shape[0] // 2, keep.shape[1]

    def kernel(keep_ref, got_ref, place_ref, keep_out, send_out, scr):
        scr[...] = (keep_ref[...].astype(F32) + got_ref[...].astype(F32)).astype(BF16)
        high = place_ref[2] // 2
        keep_out[...] = scr[pl.ds(pl.multiple_of(high * rows, rows), rows), :]
        send_out[...] = scr[pl.ds(pl.multiple_of((1 - high) * rows, rows), rows), :]

    whole = pl.BlockSpec((2 * rows, TILE), lambda j: (0, j))
    return run(
        kernel,
        (width // TILE,),
        (keep, got, place),
        [whole, whole, SMEM],
        [shape_of(rows, width)] * 2,
        [pl.BlockSpec((rows, TILE), lambda j: (0, j))] * 2,
        [pltpu.VMEM((2 * rows, TILE), BF16)],
    )


def run_col_second(run, pairs):
    sizes = [keep.shape[0] for keep, _ in pairs]
    width = pairs[0][0].shape[1]
    flat = [array for pair in pairs for array in pair]

    def kernel(*refs):
        start = 0
        for t, rows in enumerate(sizes):
            total = refs[2 * t][...].astype(F32) + refs[2 * t + 1][...].astype(F32)
            refs[-1][start : start + rows] = total.astype(BF16)
            start += rows

    return run(
        kernel,
        (width // TILE,),
        flat,
        [pl.BlockSpec((array.shape[0], TILE), lambda j: (0, j)) for array in flat],
        shape_of(sum(sizes), width),
        pl.BlockSpec((sum(sizes), TILE), lambda j: (0, j)),
    )


def run_fence(run, *arrays):
    def kernel(out_ref):
        out_ref[...] = jnp.zeros_like(out_ref)

    run.hold(*arrays)
    run(kernel, (), (), [], shape_of(16, BLOCK), pl.BlockSpec((16, BLOCK), lambda: (0, 0)))
    return run.held


def run_by_group(run, tokens, tokens_other, dy, dy_other, place):
    count, width = tokens.shape
    step = 256

    def kernel(x_ref, xo_ref, dy_ref, dyo_ref, place_ref, xt_out, dy_out):
        for x, y, group in ((x_ref, dy_ref, place_ref[1]), (xo_ref, dyo_ref, 1 - place_ref[1])):
            at = pl.ds(pl.multiple_of(group * count, count), count)
            xt_out[:, at] = x[...].T
            dy_out[at, :] = y[...]

    return run(
        kernel,
        (width // step,),
        (tokens, tokens_other, dy, dy_other, place),
        [pl.BlockSpec((count, step), lambda j: (0, j))] * 4 + [SMEM],
        [shape_of(width, 2 * count), shape_of(2 * count, width)],
        [pl.BlockSpec((step, 2 * count), lambda j: (j, 0)), pl.BlockSpec((2 * count, step), lambda j: (0, j))],
    )


def run_output(run, hiddens, down_weight, down_mask, place):
    count = hiddens[0].shape[0]
    hidden_units, width = down_weight.shape

    def kernel(*refs):
        h_refs = refs[: len(hiddens)]
        wd_ref, md_ref, place_ref, keep_ref, send_ref, scr, w_scr = refs[len(hiddens) :]
        weight = masked(w_scr, wd_ref, md_ref, 0, pl.program_id(0) * (TILE // BLOCK))
        total, at = None, 0
        for h_ref in h_refs:
            cols = h_ref.shape[1]
            term = dot(h_ref[...], weight[at : at + cols])
            total, at = term if total is None else total + term, at + cols
        write_col_halves(total, place_ref, keep_ref, send_ref, scr)

    shapes, specs, scratch = col_halves(count, width)
    return run(
        kernel,
        (width // TILE,),
        (*hiddens, down_weight, down_mask, place),
        [full(h) for h in hiddens] + [pl.BlockSpec((hidden_units, TILE), lambda j: (0, j)), SMEM, SMEM],
        shapes,
        specs,
        scratch + [pltpu.VMEM((hidden_units, TILE), BF16)],
        flops=2 * count * hidden_units * width,
    )


def weight_blocks(derivs, starts):
    return [lo // TILE + q for d, lo in zip(derivs, starts) for q in range(d.shape[1] // 2 // TILE)]


def run_token_terms(run, derivs, starts, gate_weight, up_weight, gate_mask, up_mask):
    count, width = derivs[0].shape[0], gate_weight.shape[0]
    blocks = weight_blocks(derivs, starts)
    n = len(blocks)

    def kernel(*refs):
        d_refs, weights = refs[: len(derivs)], refs[len(derivs) : len(derivs) + 2 * n]
        mg_ref, mu_ref, out_ref, w_scr = refs[len(derivs) + 2 * n :]
        row_at = pl.program_id(0) * (TILE // BLOCK)
        total, i = None, 0
        for d_ref in d_refs:
            steps = d_ref.shape[1] // 2 // TILE
            for q in range(steps):
                for part, m_ref in ((0, mg_ref), (1, mu_ref)):
                    at = part * n + i
                    weight = masked(w_scr.at[at], weights[at], m_ref, row_at, blocks[i] * (TILE // BLOCK))
                    start = (part * steps + q) * TILE
                    term = dot(d_ref[:, start : start + TILE], weight, 1, 1)
                    total = term if total is None else total + term
                i += 1
        out_ref[...] = total

    weight_specs = [pl.BlockSpec((TILE, TILE), functools.partial(lambda q, j: (j, q), q)) for q in blocks]
    return run(
        kernel,
        (width // TILE,),
        (*derivs, *[gate_weight] * n, *[up_weight] * n, gate_mask, up_mask),
        [full(d) for d in derivs] + weight_specs * 2 + [SMEM] * 2,
        jax.ShapeDtypeStruct((count, width), F32),
        pl.BlockSpec((count, TILE), lambda j: (0, j)),
        [pltpu.VMEM((2 * n, TILE, TILE), BF16)],
        flops=4 * count * n * TILE * width,
    )


def run_token_grad(run, deriv, terms, gate_weight, up_weight, gate_mask, up_mask, place, lo, t, pieces):
    count, width = terms.shape
    share = count // 4
    rows = share // pieces
    blocks = weight_blocks([deriv], [lo])
    n = len(blocks)

    def kernel(*refs):
        d_ref, terms_ref = refs[:2]
        mg_ref, mu_ref, place_ref, keep_ref, send_ref, scr, w_scr, d_scr = refs[2 + 2 * n :]
        j = pl.program_id(0)

        def gather():
            for owner in range(4):
                start = owner * share + t * rows
                d_scr[owner * rows : (owner + 1) * rows] = d_ref[start : start + rows]

        pl.when(j == 0)(gather)
        total = None
        for i in range(2 * n):
            m_ref = mg_ref if i < n else mu_ref
            weight = masked(
                w_scr.at[i], refs[2 + i], m_ref, j * (TILE // BLOCK), blocks[i % n] * (TILE // BLOCK)
            )
            term = dot(d_scr[:, i * TILE : (i + 1) * TILE], weight, 1, 1)
            total = term if total is None else total + term
        low = place_ref[2] & 1
        for owner in range(4):
            start = owner * share + t * rows
            scr[owner * rows : (owner + 1) * rows] = (
                total[owner * rows : (owner + 1) * rows] + terms_ref[start : start + rows]
            ).astype(BF16)
        for i in range(2):
            for ref, bit in ((keep_ref, low), (send_ref, 1 - low)):
                ref[i * rows : (i + 1) * rows] = scr[pl.ds(pl.multiple_of((2 * i + bit) * rows, rows), rows), :]

    shapes, specs, scratch = col_halves(4 * rows, width)
    weight_specs = [pl.BlockSpec((TILE, TILE), functools.partial(lambda q, j: (j, q), q)) for q in blocks]
    return run(
        kernel,
        (width // TILE,),
        (deriv, terms, *[gate_weight] * n, *[up_weight] * n, gate_mask, up_mask, place),
        [full(deriv), pl.BlockSpec((count, TILE), lambda j: (0, j))] + weight_specs * 2 + [SMEM] * 3,
        shapes,
        specs,
        scratch + [pltpu.VMEM((2 * n, TILE, TILE), BF16), pltpu.VMEM((4 * rows, deriv.shape[1]), BF16)],
        flops=16 * rows * n * TILE * width,
    )


def both_groups(dst, own, other, place_ref, count):
    for ref, group in ((own, place_ref[1]), (other, 1 - place_ref[1])):
        dst[pl.ds(pl.multiple_of(group * count, count), count), :] = ref[...]


def run_down_grad(run, hid, hid_other, dy_all, down_mask, place, lo, hidden_units, so_far):
    count, cols = hid.shape
    width = dy_all.shape[1]
    n, base = cols // TILE, lo // TILE
    more = [] if so_far is None else [so_far]

    def kernel(*refs):
        h_ref, ho_ref, dy_ref, md_ref, place_ref = refs[:5]
        out_ref, h_all = refs[-2:]
        j = pl.program_id(0)
        both_groups(h_all, h_ref, ho_ref, place_ref, count)
        left = h_all[...]
        for at in range(0, width, 512):
            grad = dot(left, dy_ref[:, at : at + 512], 0, 0).astype(BF16)
            store_masked(out_ref.at[:, at : at + 512], 0, grad, md_ref, (base + j) * (TILE // BLOCK), at // BLOCK)

    return run(
        kernel,
        (n,),
        (hid, hid_other, dy_all, down_mask, place, *more),
        [pl.BlockSpec((count, TILE), lambda j: (0, j))] * 2 + [full(dy_all), SMEM, SMEM] + [ANY] * len(more),
        shape_of(hidden_units, width),
        pl.BlockSpec((TILE, width), lambda j: (base + j, 0)),
        [pltpu.VMEM((2 * count, TILE), BF16)],
        flops=4 * count * width * cols,
        alias={5: 0} if more else None,
    )


def run_weight_grads(run, xt_all, deriv, deriv_other, masks, place, lo, hidden_units, so_far):
    width, all_count = xt_all.shape
    count = all_count // 2
    cols = deriv.shape[1] // 2
    n, base = cols // TILE, lo // TILE
    more = [] if so_far is None else list(so_far)

    def kernel(xt_ref, dg, du, dgo, duo, mg_ref, mu_ref, place_ref, *rest):
        gate_out, up_out, d_all = rest[-3:]
        col_at = (base + pl.program_id(0)) * (TILE // BLOCK)
        for own, other, m_ref, out in ((dg, dgo, mg_ref, gate_out), (du, duo, mu_ref, up_out)):
            both_groups(d_all, own, other, place_ref, count)
            right = d_all[...]
            for at in range(0, width, 512):
                grad = dot(xt_ref[at : at + 512], right).astype(BF16)
                store_masked(out, at, grad, m_ref, at // BLOCK, col_at)

    gate_spec = pl.BlockSpec((count, TILE), lambda j: (0, j))
    up_spec = pl.BlockSpec((count, TILE), lambda j: (0, n + j))
    return run(
        kernel,
        (n,),
        (xt_all, deriv, deriv, deriv_other, deriv_other, *masks, place, *more),
        [full(xt_all)] + [gate_spec, up_spec] * 2 + [SMEM] * 3 + [ANY] * len(more),
        [shape_of(width, hidden_units)] * 2,
        [pl.BlockSpec((width, TILE), lambda j: (0, base + j))] * 2,
        [pltpu.VMEM((all_count, TILE), BF16)],
        flops=8 * count * width * cols,
        alias={8: 0, 9: 1} if more else None,
    )


def fast_body(tokens, out_grad, gate_weight, up_weight, down_weight, gate_mask, up_mask, down_mask):
    run = Runner()
    row, dp, col = (lax.axis_index(name) for name in ("row", "dp", "col"))
    place = jnp.stack([row, dp, col]).astype(jnp.int32)
    count, width = tokens.shape
    share = count // 4
    hidden_units = gate_weight.shape[1]
    masks = (gate_mask, up_mask)
    tiles = hidden_units // TILE
    edges = [0, tiles * 2 // 7 * TILE, tiles * 5 // 7 * TILE, hidden_units]
    pieces = 2
    rows = share // pieces

    def gate_up(i):
        parts = run_gate_up(run, tokens, gate_weight, up_weight, *masks, place, edges[i], edges[i + 1])
        return parts, pair_x(parts[3]), pair_y(parts[4])

    def combine(parts, got_gate, got_up):
        one, two = run_combine(run, parts[1], parts[2], got_gate, got_up)
        return parts[0], pair_x(one), pair_y(two)

    def gather(array):
        return lax.all_gather(array, "row", axis=0, tiled=True)

    def derivs(sums, i):
        return run_derivs(run, sums, back, edges[i], 0, share)

    def down(hid, other, i, so_far):
        return run_down_grad(run, hid, other, dy_all, down_mask, place, edges[i], hidden_units, so_far)

    def weights(deriv, other, i, so_far):
        return run_weight_grads(run, xt_all, deriv, other, masks, place, edges[i], hidden_units, so_far)

    tokens_other, dy_other = swap_dp(tokens), swap_dp(out_grad)
    back = run_back(run, out_grad, down_weight, down_mask)
    back = lax.psum_scatter(back, "row", scatter_dimension=0, tiled=True)
    first = gate_up(0)
    run.after(tokens_other, dy_other)
    second = gate_up(1)
    sums_0 = combine(*first)
    third = gate_up(2)
    sums_1 = combine(*second)
    run.after(back)
    hid_0 = gather(run_hidden(run, [sums_0, sums_1]))
    sums_2 = combine(*third)
    own_1 = derivs(sums_1, 1)
    near_1 = pair_x(own_1), pair_y(own_1)
    deriv_0 = derivs(sums_0, 0)
    xt_all, dy_all = run_by_group(run, tokens, tokens_other, out_grad, dy_other, place)
    hid_2 = run_hidden(run, [sums_2])
    run.hold(hid_0, hid_2)
    deriv_2 = derivs(sums_2, 2)
    hid_0, hid_2 = run.held
    hid_2 = gather(hid_2)
    hid_0_other = swap_dp(hid_0)
    down_grad = down(hid_0, hid_0_other, 0, None)
    *near_1, hid_2, deriv_0 = run_fence(run, *near_1, hid_2, deriv_0)
    deriv_1 = gather_far(run, own_1, near_1, place)
    deriv_0 = gather(deriv_0)
    out_keep, send = run_output(run, [hid_0, hid_2], down_weight, down_mask, place)
    out_got = pair_z(send, 1)
    deriv_1 = deriv_1()
    grads = weights(deriv_1, swap_dp(deriv_1), 1, None)
    run.after(out_got)
    deriv_0, deriv_2, hid_2 = run_fence(run, deriv_0, deriv_2, hid_2)
    deriv_2 = gather(deriv_2)
    out_keep, send = run_col_first(run, out_keep, out_got, place)
    out_got = pair_z(send, 2)
    grads = weights(deriv_0, swap_dp(deriv_0), 0, grads)
    terms = run_token_terms(run, [deriv_0, deriv_1], [0, edges[1]], gate_weight, up_weight, *masks)
    run.after(out_got)
    (deriv_2,) = run_fence(run, deriv_2)
    halves = []
    for t in range(pieces):
        keep, send = run_token_grad(
            run, deriv_2, terms, gate_weight, up_weight, *masks, place, edges[2], t, pieces
        )
        halves.append((keep, pair_z(send, 1)))
    deriv_2_other = swap_dp(deriv_2)
    down_grad = down(hid_2, swap_dp(hid_2), 2, down_grad)
    pairs = []
    for keep, got in halves:
        keep, send = run_col_first(run, keep, got, place)
        pairs.append((keep, pair_z(send, 2)))
    grads = weights(deriv_2, deriv_2_other, 2, grads)
    output = run_col_second(run, [(out_keep, out_got)])
    token_grad = run_col_second(run, pairs)
    return output, token_grad, *grads, down_grad


def plain_body(
    tokens, out_grad, gate_weight, up_weight, down_weight, gate_mask, up_mask, down_mask
):
    gate_keep = expand(gate_mask)
    up_keep = expand(up_mask)
    down_keep = expand(down_mask)
    gate_eff = gate_weight * gate_keep.astype(BF16)
    up_eff = up_weight * up_keep.astype(BF16)
    down_eff = down_weight * down_keep.astype(BF16)

    def scatter(array, axis):
        return lax.psum_scatter(array.astype(BF16), axis, scatter_dimension=0, tiled=True)

    def gather(array):
        return lax.all_gather(array, "row", axis=0, tiled=True)

    gate_share = scatter(dot(tokens, gate_eff), "row").astype(F32)
    up_share = scatter(dot(tokens, up_eff), "row").astype(F32)
    gate_sig = jax.nn.sigmoid(gate_share)
    silu_gate = gate_share * gate_sig
    hidden = gather((silu_gate * up_share).astype(BF16))
    output = scatter(dot(hidden, down_eff), "col")
    down_local = contract_rows(hidden, out_grad) * down_keep.astype(F32)
    back_share = scatter(contract_cols(out_grad, down_eff), "row").astype(F32)
    gate_deriv = back_share * up_share * gate_sig * (1.0 + gate_share * (1.0 - gate_sig))
    gate_full = gather(gate_deriv.astype(BF16))
    up_full = gather((back_share * silu_gate).astype(BF16))
    token_grad = scatter(contract_cols(gate_full, gate_eff) + contract_cols(up_full, up_eff), "col")
    gate_local = contract_rows(tokens, gate_full) * gate_keep.astype(F32)
    up_local = contract_rows(tokens, up_full) * up_keep.astype(F32)
    totals = [
        lax.psum(local.astype(BF16), "dp") for local in (gate_local, up_local, down_local)
    ]
    return (output, token_grad, *totals)


def solution(mesh):
    wide, tall = P("row", "col"), P("col", "row")
    tok, spread = P("dp", "row"), P(("dp", "col"), "row")
    body = plain_body
    if mesh.shape["row"] == 4 and mesh.shape["dp"] == 2 and mesh.shape["col"] == 4:
        body = fast_body
    return jax.shard_map(
        body,
        mesh=mesh,
        in_specs=(tok, tok, wide, wide, tall, wide, wide, tall),
        out_specs=(spread, spread, wide, wide, tall),
        check_vma=False,
    )
```

```python
import functools
import inspect

import jax
import jax.numpy as jnp
from jax import lax
from jax.experimental import pallas as pl
from jax.experimental.pallas import tpu as pltpu
from jax.sharding import PartitionSpec as P

BLOCK = 128
TILE = 512
F32 = jnp.float32
BF16 = jnp.bfloat16
ANY = pl.BlockSpec(memory_space=pl.ANY)
SMEM = pl.BlockSpec(memory_space=pltpu.SMEM)


def expand(mask_tile):
    return jnp.repeat(jnp.repeat(mask_tile, BLOCK, axis=0), BLOCK, axis=1)


def dot(left_side, right_side, left_dim=1, right_dim=0):
    return lax.dot_general(
        left_side, right_side, (((left_dim,), (right_dim,)), ((), ())), preferred_element_type=F32
    )


def contract_rows(left_side, right_side):
    return dot(left_side, right_side, 0, 0)


def contract_cols(left_side, right_side):
    return dot(left_side, right_side, 1, 1)


def pair_x(array):
    return lax.ppermute(array, "row", [(i, i ^ 1) for i in range(4)])


def pair_y(array):
    return lax.ppermute(array, "row", [(i, i ^ 2) for i in range(4)])


def pair_z(array, bit):
    return lax.ppermute(array, "col", [(i, i ^ bit) for i in range(4)])


def swap_dp(array):
    return lax.ppermute(array, "dp", [(0, 1), (1, 0)])


def cat(parts, axis=0):
    return lax.concatenate(parts, axis)


def shape_of(*dims):
    return jax.ShapeDtypeStruct(dims, BF16)


def full(array):
    return pl.BlockSpec(array.shape, lambda *at: (0,) * array.ndim)


class Runner:
    def __init__(self):
        self.last, self.count = None, 0
        self.waits, self.held = (), ()

    def after(self, *arrays):
        self.waits = arrays

    def hold(self, *arrays):
        self.holding = arrays

    holding = ()

    def __call__(self, kernel, grid, args, in_specs, out_shape, out_specs, scratch=(), flops=0, alias=None):
        name = "k%02d_%s" % (self.count, inspect.stack()[1].function[4:])
        self.count += 1
        single = not isinstance(out_shape, (tuple, list))
        out_shape = [out_shape] if single else list(out_shape)
        out_specs = [out_specs] if single else list(out_specs)
        last = [] if self.last is None else [self.last]
        holding = list(self.holding)
        extra = [*last, *self.waits, *holding]
        self.waits, self.holding = (), ()
        count, outs = len(args), len(out_shape)
        alias = dict(alias or {})
        for i in range(len(holding)):
            alias[count + len(extra) - len(holding) + i] = outs + i

        def wrapped(*refs):
            rest = refs[count + len(extra) :]
            kernel(*refs[:count], *rest[:outs], *rest[outs + len(holding) :])

        results = pl.pallas_call(
            wrapped,
            name=name,
            grid=grid,
            in_specs=list(in_specs) + [ANY] * len(extra),
            out_specs=out_specs + [ANY] * len(holding),
            out_shape=out_shape + [jax.ShapeDtypeStruct(a.shape, a.dtype) for a in holding],
            scratch_shapes=list(scratch),
            input_output_aliases=alias,
            compiler_params=pltpu.CompilerParams(vmem_limit_bytes=56 * 1024 * 1024),
            cost_estimate=pl.CostEstimate(flops=flops // (4 if 'terms' in name else 1), bytes_accessed=1 << 22, transcendentals=0),
        )(*args, *extra)
        self.last = results[0]
        self.held = tuple(results[outs:])
        return results[0] if single else results[:outs]


def masked(scr, weight_ref, mask_ref, row_at, col_at):
    rows, cols = weight_ref.shape
    for r in range(rows // BLOCK):
        for c in range(cols // BLOCK):
            at = (slice(r * BLOCK, (r + 1) * BLOCK), slice(c * BLOCK, (c + 1) * BLOCK))
            tile = weight_ref[at]
            scr[at] = jnp.where(mask_ref[row_at + r, col_at + c] > 0, tile, jnp.zeros_like(tile))
    return scr[...]


def store_masked(out_ref, row, grad, mask_ref, row_at, col_at):
    rows, cols = grad.shape
    for r in range(0, rows, BLOCK):
        for c in range(0, cols, BLOCK):
            tile = grad[r : r + BLOCK, c : c + BLOCK]
            kept = mask_ref[row_at + r // BLOCK, col_at + c // BLOCK] > 0
            out_ref[row + r : row + r + BLOCK, c : c + BLOCK] = jnp.where(kept, tile, jnp.zeros_like(tile))


def run_gate_up(run, tokens, gate_weight, up_weight, gate_mask, up_mask, place, lo, hi):
    count, width = tokens.shape
    n, base, share, cols = (hi - lo) // TILE, lo // TILE, count // 4, hi - lo

    def kernel(x_ref, wg_ref, wu_ref, mg_ref, mu_ref, place_ref, s0, s1, s2, g3, u3, w_scr, scr):
        part, j = pl.program_id(0), pl.program_id(1)

        def work(w_ref, m_ref, last):
            weight = masked(w_scr, w_ref, m_ref, 0, (base + j) * (TILE // BLOCK))
            scr[...] = dot(x_ref[...], weight).astype(BF16)
            for k, out in enumerate((s0, s1, s2, last)):
                out[...] = scr[pl.ds(pl.multiple_of((place_ref[0] ^ k) * share, share), share), :]

        pl.when(part == 0)(lambda: work(wg_ref, mg_ref, g3))
        pl.when(part == 1)(lambda: work(wu_ref, mu_ref, u3))

    def first(p, j):
        return (0, jnp.where(p == 0, j, n - 1))

    def second(p, j):
        return (0, jnp.where(p == 0, 0, j))

    both = pl.BlockSpec((share, TILE), lambda p, j: (0, p * n + j))
    return run(
        kernel,
        (2, n),
        (tokens, gate_weight, up_weight, gate_mask, up_mask, place),
        [
            full(tokens),
            pl.BlockSpec((width, TILE), lambda p, j: (0, base + jnp.where(p == 0, j, n - 1))),
            pl.BlockSpec((width, TILE), lambda p, j: (0, base + jnp.where(p == 0, 0, j))),
            SMEM,
            SMEM,
            SMEM,
        ],
        [shape_of(share, 2 * cols)] * 3 + [shape_of(share, cols)] * 2,
        [both] * 3 + [pl.BlockSpec((share, TILE), first), pl.BlockSpec((share, TILE), second)],
        [pltpu.VMEM((width, TILE), BF16), pltpu.VMEM((count, TILE), BF16)],
        flops=4 * count * width * cols,
    )


def run_combine(run, one, two, got_gate, got_up):
    share, cols = got_up.shape

    def kernel(one_ref, two_ref, gate_ref, up_ref, one_out, two_out):
        one_out[...] = (one_ref[...].astype(F32) + up_ref[...].astype(F32)).astype(BF16)
        two_out[...] = (two_ref[...].astype(F32) + gate_ref[...].astype(F32)).astype(BF16)

    rows = share // 2
    low = pl.BlockSpec((rows, cols), lambda j: (j, 0))
    high = pl.BlockSpec((rows, cols), lambda j: (j, 1))
    return run(
        kernel,
        (2,),
        (one, two, got_gate, got_up),
        [high, low, low, low],
        [shape_of(*one.shape)] * 2,
        [high, low],
        alias={0: 0, 1: 1},
    )


def run_back(run, out_grad, down_weight, down_mask):
    count, width = out_grad.shape
    hidden_units = down_weight.shape[0]

    def kernel(dy_ref, wd_ref, md_ref, out_ref, w_scr):
        weight = masked(w_scr, wd_ref, md_ref, pl.program_id(0) * (TILE // BLOCK), 0)
        out_ref[...] = dot(dy_ref[...], weight, 1, 1).astype(BF16)

    return run(
        kernel,
        (hidden_units // TILE,),
        (out_grad, down_weight, down_mask),
        [full(out_grad), pl.BlockSpec((TILE, width), lambda j: (j, 0)), SMEM],
        shape_of(count, hidden_units),
        pl.BlockSpec((count, TILE), lambda j: (0, j)),
        [pltpu.VMEM((TILE, width), BF16)],
        flops=2 * count * width * hidden_units,
    )


def add_three(refs, col, width):
    first, second, third = (ref[:, col : col + width].astype(F32) for ref in refs)
    return first + second + third


STEP = 256


def run_hidden(run, sums):
    share = sums[0][0].shape[0]
    widths = [group[0].shape[1] // 2 for group in sums]
    rows = share // 6

    def kernel(*refs):
        out_ref, start = refs[-1], 0
        for i, cols in enumerate(widths):
            group = refs[3 * i : 3 * i + 3]
            for at in range(0, cols, STEP):
                gate, up = add_three(group, at, STEP), add_three(group, cols + at, STEP)
                out_ref[:, start + at : start + at + STEP] = (gate * jax.nn.sigmoid(gate) * up).astype(BF16)
            start += cols

    flat = [array for group in sums for array in group]
    return run(
        kernel,
        (share // rows,),
        flat,
        [pl.BlockSpec((rows, array.shape[1]), lambda j: (j, 0)) for array in flat],
        shape_of(share, sum(widths)),
        pl.BlockSpec((rows, sum(widths)), lambda j: (j, 0)),
    )


def run_derivs(run, sums, back, back_at, row_lo, row_hi):
    cols = sums[0].shape[1] // 2
    rows = 32
    base = row_lo // rows

    def kernel(s0, s1, s2, back_ref, out_ref):
        for at in range(0, cols, STEP):
            gate, up = add_three((s0, s1, s2), at, STEP), add_three((s0, s1, s2), cols + at, STEP)
            grad = back_ref[:, at : at + STEP].astype(F32)
            sig = jax.nn.sigmoid(gate)
            silu = gate * sig
            out_ref[:, at : at + STEP] = (grad * up * (sig + silu * (1.0 - sig))).astype(BF16)
            out_ref[:, cols + at : cols + at + STEP] = (grad * silu).astype(BF16)

    return run(
        kernel,
        ((row_hi - row_lo) // rows,),
        (*sums, back),
        [pl.BlockSpec((rows, 2 * cols), lambda j: (base + j, 0))] * 3
        + [pl.BlockSpec((pl.Element(rows), pl.Element(cols)), lambda j: ((base + j) * rows, back_at))],
        shape_of(row_hi - row_lo, 2 * cols),
        pl.BlockSpec((rows, 2 * cols), lambda j: (j, 0)),
    )


def run_assemble(run, parts, place):
    rows, width = parts[0].shape
    half = rows // 2

    def kernel(*refs):
        place_ref, out_ref = refs[5], refs[6]
        for k, part in enumerate(refs[:5]):
            at = (place_ref[0] ^ min(k, 3)) * rows + (half if k == 4 else 0)
            out_ref[pl.ds(pl.multiple_of(at, half), part.shape[0]), :] = part[...]

    return run(
        kernel,
        (width // TILE,),
        (*parts, place),
        [pl.BlockSpec((part.shape[0], TILE), lambda j: (0, j)) for part in parts] + [SMEM],
        shape_of(4 * rows, width),
        pl.BlockSpec((4 * rows, TILE), lambda j: (0, j)),
    )


def gather_far(run, own, got, place):
    half = own.shape[0] // 2
    far = [pair_y(got[0][:half]), pair_x(got[1][half:])]
    return lambda: run_assemble(run, (own, *got, *far), place)


def write_col_halves(total, place_ref, keep_ref, send_ref, scr):
    rows = total.shape[0] // 4
    scr[...] = total.astype(BF16)
    low = place_ref[2] & 1
    for i in range(2):
        keep_ref[i * rows : (i + 1) * rows] = scr[pl.ds(pl.multiple_of((2 * i + low) * rows, rows), rows), :]
        send_ref[i * rows : (i + 1) * rows] = scr[pl.ds(pl.multiple_of((2 * i + 1 - low) * rows, rows), rows), :]


def col_halves(count, width):
    spec = pl.BlockSpec((count // 2, TILE), lambda j: (0, j))
    return [shape_of(count // 2, width)] * 2, [spec] * 2, [pltpu.VMEM((count, TILE), BF16)]


def run_col_first(run, keep, got, place):
    rows, width = keep.shape[0] // 2, keep.shape[1]

    def kernel(keep_ref, got_ref, place_ref, keep_out, send_out, scr):
        scr[...] = (keep_ref[...].astype(F32) + got_ref[...].astype(F32)).astype(BF16)
        high = place_ref[2] // 2
        keep_out[...] = scr[pl.ds(pl.multiple_of(high * rows, rows), rows), :]
        send_out[...] = scr[pl.ds(pl.multiple_of((1 - high) * rows, rows), rows), :]

    whole = pl.BlockSpec((2 * rows, TILE), lambda j: (0, j))
    return run(
        kernel,
        (width // TILE,),
        (keep, got, place),
        [whole, whole, SMEM],
        [shape_of(rows, width)] * 2,
        [pl.BlockSpec((rows, TILE), lambda j: (0, j))] * 2,
        [pltpu.VMEM((2 * rows, TILE), BF16)],
    )


def run_col_second(run, pairs):
    sizes = [keep.shape[0] for keep, _ in pairs]
    width = pairs[0][0].shape[1]
    flat = [array for pair in pairs for array in pair]

    def kernel(*refs):
        start = 0
        for t, rows in enumerate(sizes):
            total = refs[2 * t][...].astype(F32) + refs[2 * t + 1][...].astype(F32)
            refs[-1][start : start + rows] = total.astype(BF16)
            start += rows

    return run(
        kernel,
        (width // TILE,),
        flat,
        [pl.BlockSpec((array.shape[0], TILE), lambda j: (0, j)) for array in flat],
        shape_of(sum(sizes), width),
        pl.BlockSpec((sum(sizes), TILE), lambda j: (0, j)),
    )


def run_fence(run, *arrays):
    def kernel(out_ref):
        out_ref[...] = jnp.zeros_like(out_ref)

    run.hold(*arrays)
    run(kernel, (), (), [], shape_of(16, BLOCK), pl.BlockSpec((16, BLOCK), lambda: (0, 0)))
    return run.held


def run_by_group(run, tokens, tokens_other, dy, dy_other, place):
    count, width = tokens.shape
    step = 256

    def kernel(x_ref, xo_ref, dy_ref, dyo_ref, place_ref, xt_out, dy_out):
        for x, y, group in ((x_ref, dy_ref, place_ref[1]), (xo_ref, dyo_ref, 1 - place_ref[1])):
            at = pl.ds(pl.multiple_of(group * count, count), count)
            xt_out[:, at] = x[...].T
            dy_out[at, :] = y[...]

    return run(
        kernel,
        (width // step,),
        (tokens, tokens_other, dy, dy_other, place),
        [pl.BlockSpec((count, step), lambda j: (0, j))] * 4 + [SMEM],
        [shape_of(width, 2 * count), shape_of(2 * count, width)],
        [pl.BlockSpec((step, 2 * count), lambda j: (j, 0)), pl.BlockSpec((2 * count, step), lambda j: (0, j))],
    )


def run_output(run, hiddens, down_weight, down_mask, place):
    count = hiddens[0].shape[0]
    hidden_units, width = down_weight.shape

    def kernel(*refs):
        h_refs = refs[: len(hiddens)]
        wd_ref, md_ref, place_ref, keep_ref, send_ref, scr, w_scr = refs[len(hiddens) :]
        weight = masked(w_scr, wd_ref, md_ref, 0, pl.program_id(0) * (TILE // BLOCK))
        total, at = None, 0
        for h_ref in h_refs:
            cols = h_ref.shape[1]
            term = dot(h_ref[...], weight[at : at + cols])
            total, at = term if total is None else total + term, at + cols
        write_col_halves(total, place_ref, keep_ref, send_ref, scr)

    shapes, specs, scratch = col_halves(count, width)
    return run(
        kernel,
        (width // TILE,),
        (*hiddens, down_weight, down_mask, place),
        [full(h) for h in hiddens] + [pl.BlockSpec((hidden_units, TILE), lambda j: (0, j)), SMEM, SMEM],
        shapes,
        specs,
        scratch + [pltpu.VMEM((hidden_units, TILE), BF16)],
        flops=2 * count * hidden_units * width,
    )


def weight_blocks(derivs, starts):
    return [lo // TILE + q for d, lo in zip(derivs, starts) for q in range(d.shape[1] // 2 // TILE)]


def run_token_terms(run, derivs, starts, gate_weight, up_weight, gate_mask, up_mask):
    count, width = derivs[0].shape[0], gate_weight.shape[0]
    blocks = weight_blocks(derivs, starts)
    n = len(blocks)

    def kernel(*refs):
        d_refs, weights = refs[: len(derivs)], refs[len(derivs) : len(derivs) + 2 * n]
        mg_ref, mu_ref, out_ref, w_scr = refs[len(derivs) + 2 * n :]
        row_at = pl.program_id(0) * (TILE // BLOCK)
        total, i = None, 0
        for d_ref in d_refs:
            steps = d_ref.shape[1] // 2 // TILE
            for q in range(steps):
                for part, m_ref in ((0, mg_ref), (1, mu_ref)):
                    at = part * n + i
                    weight = masked(w_scr.at[at], weights[at], m_ref, row_at, blocks[i] * (TILE // BLOCK))
                    start = (part * steps + q) * TILE
                    term = dot(d_ref[:, start : start + TILE], weight, 1, 1)
                    total = term if total is None else total + term
                i += 1
        out_ref[...] = total

    weight_specs = [pl.BlockSpec((TILE, TILE), functools.partial(lambda q, j: (j, q), q)) for q in blocks]
    return run(
        kernel,
        (width // TILE,),
        (*derivs, *[gate_weight] * n, *[up_weight] * n, gate_mask, up_mask),
        [full(d) for d in derivs] + weight_specs * 2 + [SMEM] * 2,
        jax.ShapeDtypeStruct((count, width), F32),
        pl.BlockSpec((count, TILE), lambda j: (0, j)),
        [pltpu.VMEM((2 * n, TILE, TILE), BF16)],
        flops=4 * count * n * TILE * width,
    )


def run_token_grad(run, deriv, terms, gate_weight, up_weight, gate_mask, up_mask, place, lo, t, pieces):
    count, width = terms.shape
    share = count // 4
    rows = share // pieces
    blocks = weight_blocks([deriv], [lo])
    n = len(blocks)

    def kernel(*refs):
        d_ref, terms_ref = refs[:2]
        mg_ref, mu_ref, place_ref, keep_ref, send_ref, scr, w_scr, d_scr = refs[2 + 2 * n :]
        j = pl.program_id(0)

        def gather():
            for owner in range(4):
                start = owner * share + t * rows
                d_scr[owner * rows : (owner + 1) * rows] = d_ref[start : start + rows]

        pl.when(j == 0)(gather)
        total = None
        for i in range(2 * n):
            m_ref = mg_ref if i < n else mu_ref
            weight = masked(
                w_scr.at[i], refs[2 + i], m_ref, j * (TILE // BLOCK), blocks[i % n] * (TILE // BLOCK)
            )
            term = dot(d_scr[:, i * TILE : (i + 1) * TILE], weight, 1, 1)
            total = term if total is None else total + term
        low = place_ref[2] & 1
        for owner in range(4):
            start = owner * share + t * rows
            scr[owner * rows : (owner + 1) * rows] = (
                total[owner * rows : (owner + 1) * rows] + terms_ref[start : start + rows]
            ).astype(BF16)
        for i in range(2):
            for ref, bit in ((keep_ref, low), (send_ref, 1 - low)):
                ref[i * rows : (i + 1) * rows] = scr[pl.ds(pl.multiple_of((2 * i + bit) * rows, rows), rows), :]

    shapes, specs, scratch = col_halves(4 * rows, width)
    weight_specs = [pl.BlockSpec((TILE, TILE), functools.partial(lambda q, j: (j, q), q)) for q in blocks]
    return run(
        kernel,
        (width // TILE,),
        (deriv, terms, *[gate_weight] * n, *[up_weight] * n, gate_mask, up_mask, place),
        [full(deriv), pl.BlockSpec((count, TILE), lambda j: (0, j))] + weight_specs * 2 + [SMEM] * 3,
        shapes,
        specs,
        scratch + [pltpu.VMEM((2 * n, TILE, TILE), BF16), pltpu.VMEM((4 * rows, deriv.shape[1]), BF16)],
        flops=16 * rows * n * TILE * width,
    )


def both_groups(dst, own, other, place_ref, count):
    for ref, group in ((own, place_ref[1]), (other, 1 - place_ref[1])):
        dst[pl.ds(pl.multiple_of(group * count, count), count), :] = ref[...]


def run_down_grad(run, hid, hid_other, dy_all, down_mask, place, lo, hidden_units, so_far):
    count, cols = hid.shape
    width = dy_all.shape[1]
    n, base = cols // TILE, lo // TILE
    more = [] if so_far is None else [so_far]

    def kernel(*refs):
        h_ref, ho_ref, dy_ref, md_ref, place_ref = refs[:5]
        out_ref, h_all = refs[-2:]
        j = pl.program_id(0)
        both_groups(h_all, h_ref, ho_ref, place_ref, count)
        left = h_all[...]
        for at in range(0, width, 512):
            grad = dot(left, dy_ref[:, at : at + 512], 0, 0).astype(BF16)
            store_masked(out_ref.at[:, at : at + 512], 0, grad, md_ref, (base + j) * (TILE // BLOCK), at // BLOCK)

    return run(
        kernel,
        (n,),
        (hid, hid_other, dy_all, down_mask, place, *more),
        [pl.BlockSpec((count, TILE), lambda j: (0, j))] * 2 + [full(dy_all), SMEM, SMEM] + [ANY] * len(more),
        shape_of(hidden_units, width),
        pl.BlockSpec((TILE, width), lambda j: (base + j, 0)),
        [pltpu.VMEM((2 * count, TILE), BF16)],
        flops=4 * count * width * cols,
        alias={5: 0} if more else None,
    )


def run_weight_grads(run, xt_all, deriv, deriv_other, masks, place, lo, hidden_units, so_far):
    width, all_count = xt_all.shape
    count = all_count // 2
    cols = deriv.shape[1] // 2
    n, base = cols // TILE, lo // TILE
    more = [] if so_far is None else list(so_far)

    def kernel(xt_ref, dg, du, dgo, duo, mg_ref, mu_ref, place_ref, *rest):
        gate_out, up_out, d_all = rest[-3:]
        col_at = (base + pl.program_id(0)) * (TILE // BLOCK)
        for own, other, m_ref, out in ((dg, dgo, mg_ref, gate_out), (du, duo, mu_ref, up_out)):
            both_groups(d_all, own, other, place_ref, count)
            right = d_all[...]
            for at in range(0, width, 512):
                grad = dot(xt_ref[at : at + 512], right).astype(BF16)
                store_masked(out, at, grad, m_ref, at // BLOCK, col_at)

    gate_spec = pl.BlockSpec((count, TILE), lambda j: (0, j))
    up_spec = pl.BlockSpec((count, TILE), lambda j: (0, n + j))
    return run(
        kernel,
        (n,),
        (xt_all, deriv, deriv, deriv_other, deriv_other, *masks, place, *more),
        [full(xt_all)] + [gate_spec, up_spec] * 2 + [SMEM] * 3 + [ANY] * len(more),
        [shape_of(width, hidden_units)] * 2,
        [pl.BlockSpec((width, TILE), lambda j: (0, base + j))] * 2,
        [pltpu.VMEM((all_count, TILE), BF16)],
        flops=8 * count * width * cols,
        alias={8: 0, 9: 1} if more else None,
    )


def fast_body(tokens, out_grad, gate_weight, up_weight, down_weight, gate_mask, up_mask, down_mask):
    run = Runner()
    row, dp, col = (lax.axis_index(name) for name in ("row", "dp", "col"))
    place = jnp.stack([row, dp, col]).astype(jnp.int32)
    count, width = tokens.shape
    share = count // 4
    hidden_units = gate_weight.shape[1]
    masks = (gate_mask, up_mask)
    tiles = hidden_units // TILE
    edges = [0, tiles * 2 // 7 * TILE, tiles * 5 // 7 * TILE, hidden_units]
    pieces = 2
    rows = share // pieces

    def gate_up(i):
        parts = run_gate_up(run, tokens, gate_weight, up_weight, *masks, place, edges[i], edges[i + 1])
        return parts, pair_x(parts[3]), pair_y(parts[4])

    def combine(parts, got_gate, got_up):
        one, two = run_combine(run, parts[1], parts[2], got_gate, got_up)
        return parts[0], pair_x(one), pair_y(two)

    def gather(array):
        return lax.all_gather(array, "row", axis=0, tiled=True)

    def derivs(sums, i):
        return run_derivs(run, sums, back, edges[i], 0, share)

    def down(hid, other, i, so_far):
        return run_down_grad(run, hid, other, dy_all, down_mask, place, edges[i], hidden_units, so_far)

    def weights(deriv, other, i, so_far):
        return run_weight_grads(run, xt_all, deriv, other, masks, place, edges[i], hidden_units, so_far)

    tokens_other, dy_other = swap_dp(tokens), swap_dp(out_grad)
    back = run_back(run, out_grad, down_weight, down_mask)
    back = lax.psum_scatter(back, "row", scatter_dimension=0, tiled=True)
    first = gate_up(0)
    run.after(tokens_other, dy_other)
    second = gate_up(1)
    sums_0 = combine(*first)
    third = gate_up(2)
    run.after(*sums_0[1:])
    sums_1 = combine(*second)
    run.after(back)
    hid_0 = gather(run_hidden(run, [sums_0, sums_1]))
    sums_2 = combine(*third)
    own_1 = derivs(sums_1, 1)
    near_1 = pair_x(own_1), pair_y(own_1)
    deriv_0 = derivs(sums_0, 0)
    xt_all, dy_all = run_by_group(run, tokens, tokens_other, out_grad, dy_other, place)
    hid_2 = run_hidden(run, [sums_2])
    run.hold(hid_0, hid_2)
    deriv_2 = derivs(sums_2, 2)
    hid_0, hid_2 = run.held
    hid_2 = gather(hid_2)
    hid_0_other = swap_dp(hid_0)
    down_grad = down(hid_0, hid_0_other, 0, None)
    *near_1, hid_2, deriv_0 = run_fence(run, *near_1, hid_2, deriv_0)
    deriv_1 = gather_far(run, own_1, near_1, place)
    deriv_0 = gather(deriv_0)
    out_keep, send = run_output(run, [hid_0, hid_2], down_weight, down_mask, place)
    out_got = pair_z(send, 1)
    deriv_1 = deriv_1()
    grads = weights(deriv_1, swap_dp(deriv_1), 1, None)
    run.after(out_got)
    deriv_0, deriv_2, hid_2 = run_fence(run, deriv_0, deriv_2, hid_2)
    deriv_2 = gather(deriv_2)
    out_keep, send = run_col_first(run, out_keep, out_got, place)
    out_got = pair_z(send, 2)
    grads = weights(deriv_0, swap_dp(deriv_0), 0, grads)
    terms = run_token_terms(run, [deriv_0, deriv_1], [0, edges[1]], gate_weight, up_weight, *masks)
    run.after(out_got)
    (deriv_2,) = run_fence(run, deriv_2)
    halves = []
    for t in range(pieces):
        keep, send = run_token_grad(
            run, deriv_2, terms, gate_weight, up_weight, *masks, place, edges[2], t, pieces
        )
        halves.append((keep, pair_z(send, 1)))
    deriv_2_other = swap_dp(deriv_2)
    down_grad = down(hid_2, swap_dp(hid_2), 2, down_grad)
    pairs = []
    for keep, got in halves:
        keep, send = run_col_first(run, keep, got, place)
        pairs.append((keep, pair_z(send, 2)))
    grads = weights(deriv_2, deriv_2_other, 2, grads)
    output = run_col_second(run, [(out_keep, out_got)])
    token_grad = run_col_second(run, pairs)
    return output, token_grad, *grads, down_grad


def plain_body(
    tokens, out_grad, gate_weight, up_weight, down_weight, gate_mask, up_mask, down_mask
):
    gate_keep = expand(gate_mask)
    up_keep = expand(up_mask)
    down_keep = expand(down_mask)
    gate_eff = gate_weight * gate_keep.astype(BF16)
    up_eff = up_weight * up_keep.astype(BF16)
    down_eff = down_weight * down_keep.astype(BF16)

    def scatter(array, axis):
        return lax.psum_scatter(array.astype(BF16), axis, scatter_dimension=0, tiled=True)

    def gather(array):
        return lax.all_gather(array, "row", axis=0, tiled=True)

    gate_share = scatter(dot(tokens, gate_eff), "row").astype(F32)
    up_share = scatter(dot(tokens, up_eff), "row").astype(F32)
    gate_sig = jax.nn.sigmoid(gate_share)
    silu_gate = gate_share * gate_sig
    hidden = gather((silu_gate * up_share).astype(BF16))
    output = scatter(dot(hidden, down_eff), "col")
    down_local = contract_rows(hidden, out_grad) * down_keep.astype(F32)
    back_share = scatter(contract_cols(out_grad, down_eff), "row").astype(F32)
    gate_deriv = back_share * up_share * gate_sig * (1.0 + gate_share * (1.0 - gate_sig))
    gate_full = gather(gate_deriv.astype(BF16))
    up_full = gather((back_share * silu_gate).astype(BF16))
    token_grad = scatter(contract_cols(gate_full, gate_eff) + contract_cols(up_full, up_eff), "col")
    gate_local = contract_rows(tokens, gate_full) * gate_keep.astype(F32)
    up_local = contract_rows(tokens, up_full) * up_keep.astype(F32)
    totals = [
        lax.psum(local.astype(BF16), "dp") for local in (gate_local, up_local, down_local)
    ]
    return (output, token_grad, *totals)


def solution(mesh):
    wide, tall = P("row", "col"), P("col", "row")
    tok, spread = P("dp", "row"), P(("dp", "col"), "row")
    body = plain_body
    if mesh.shape["row"] == 4 and mesh.shape["dp"] == 2 and mesh.shape["col"] == 4:
        body = fast_body
    return jax.shard_map(
        body,
        mesh=mesh,
        in_specs=(tok, tok, wide, wide, tall, wide, wide, tall),
        out_specs=(spread, spread, wide, wide, tall),
        check_vma=False,
    )
```
